128 devices in a mesh: comm: 16 (over z, y), inner: 8 (over x, core).
Axes of the slice: x: 4, y: 4, z: 4, core: 2. Of those that a mesh axis runs over, the one named last changes fastest.
Arguments:
- vec_x: bfloat16 [32, 524288], P(None, ('comm', 'inner')), may hold values from -8 to 8
- vec_p: bfloat16 [32, 524288], P(None, ('comm', 'inner')), may hold values from -3 to 3
- diag_shift: float32 [524288], P(('comm', 'inner')), may hold values from 0.5 to 4
- tiles: bfloat16 [24576, 256, 256], P(('comm', 'inner')), may hold values from 0 to 0.125
- tile_row: int32 [24576], P(('comm', 'inner')), may hold values from 0 to 15
- tile_col: int32 [24576], P(('comm', 'inner')), may hold values from 0 to 207
- tile_count: int32 [128], P(('comm', 'inner')), may hold values from 96 to 192, as said below
- send_near: int32 [128, 8, 8], P(('comm', 'inner')), may hold values from 0 to 15
- send_far: int32 [128, 128, 1], P(('comm', 'inner')), may hold values from 0 to 15
Outputs:
- next_x: float32 [32, 524288], P(None, ('comm', 'inner'))
- next_p: float32 [32, 524288], P(None, ('comm', 'inner'))
The draws below stay inside these ranges and needn't reach their ends.
Inputs may be any that keep to these rules, and one draw needn't show every extreme that they name: `tile_count`: some device has all 192 slots live and some exactly 96.
All inputs are finite; a program needn't handle non-finite values.
Results may differ from the reference program's by a relative error of at most 0.0046.
Values may be sent and summed in bfloat16 or wider, within the bound.
No kernel may reach another device: no remote copies, remote signals or barrier semaphores. Data moves between devices by JAX's collectives and lax.ppermute only.
A program may use at most 128 MiB of HBM per device.

```python
import math
import jax
import jax.numpy as jnp
from jax import lax

K = 32
BLK = 256
RB = 16
NT = 192
CI = 8
CC = 1
NS = 6
NROWS = 524288
POOL = 208
N_INNER = 8
DEVICES = 128


def draw_tile_count(key, part):
    key = jax.random.fold_in(key, 7)
    first, second = jax.random.split(key)
    counts = jax.random.randint(first, (DEVICES,), NT // 2, NT + 1)
    where = jax.random.randint(second, (), 0, DEVICES)
    counts = counts.at[where].set(NT)
    counts = counts.at[(where + 1) % DEVICES].set(NT // 2)
    return counts.astype(jnp.int32)


def draw_tiles(key, part):
    key = jax.random.fold_in(key, 9)
    density = 8.0 / BLK
    height = RB / NT
    level = jax.random.uniform(key, (DEVICES * NT, BLK, BLK), jnp.float32)
    within = jnp.minimum(level / density, 0.999)
    values = jnp.where(level < density, height * (0.5 + within), 0.0)
    return values.astype(jnp.bfloat16)


def draw_vec_x(key, part):
    key = jax.random.fold_in(key, 11)
    first, second = jax.random.split(key, 2)
    span = RB * BLK
    common = jax.random.normal(first, (K, DEVICES), jnp.float32)
    common = jnp.repeat(common, span, axis=1)
    noise = jax.random.normal(second, (K, NROWS), jnp.float32)
    values = 0.8 * common + 0.6 * noise
    return jnp.clip(values, -8.0, 8.0).astype(jnp.bfloat16)


def place_ends(drawn, rng, least, high):
    place = [jax.random.randint(jax.random.fold_in(rng, axis), (), 0, length) for axis, length in enumerate(drawn.shape)]
    widest = drawn.shape.index(max(drawn.shape))
    beside = place[:widest] + [(place[widest] + 1) % drawn.shape[widest]] + place[widest + 1:]
    return drawn.at[tuple(place)].set(least).at[tuple(beside)].set(high)


def steps_of(key, shape, pieces, least, top_value):
    loudness, own = 1.0, jax.random.fold_in(key, 6)
    for dim, parts in pieces:
        heights = jnp.exp(jax.random.uniform(jax.random.fold_in(own, dim), (parts,), jnp.float32, least / len(pieces), top_value / len(pieces)))
        loudness = loudness * jnp.repeat(heights, shape[dim] // parts).reshape([-1 if axis == dim else 1 for axis in range(len(shape))])
    return loudness


def normal_values(rng, shape, deviation, reach, cuts=(), kind=jnp.bfloat16):
    gain = steps_of(rng, shape, cuts, -0.22, 0.18) if cuts else 1.0
    result = jax.random.normal(rng, shape, jnp.float32) * deviation * gain
    return jnp.minimum(jnp.maximum(result, -reach), reach).astype(kind)


def setup_inputs(seed: int = 0) -> dict:
    keys = jax.random.split(jax.random.key(seed), 10)
    vec_x = draw_vec_x(jax.random.fold_in(keys[9], 71), 0)
    vec_p = normal_values(keys[1], (K, NROWS), 0.5, 3.0, ((1, 128),))
    diag_shift = jnp.clip(jnp.exp(math.log(4.0) - 2.0794415 * jax.random.uniform(keys[2], (NROWS,), jnp.float32) ** steps_of(keys[2], (NROWS,), ((0, 128),), -0.2, 0.2)), 0.5, 4.0)
    tiles = draw_tiles(jax.random.fold_in(keys[9], 71), 0)
    tile_row = place_ends(jax.random.randint(keys[4], (DEVICES * NT,), 0, RB), jax.random.fold_in(keys[4], 1), 0, RB - 1).astype(jnp.int32)
    tile_col = place_ends(jax.random.randint(keys[5], (DEVICES * NT,), 0, POOL), jax.random.fold_in(keys[5], 1), 0, POOL - 1).astype(jnp.int32)
    tile_count = draw_tile_count(jax.random.fold_in(keys[9], 71), 0)
    send_near = place_ends(jax.random.randint(keys[7], (DEVICES, N_INNER, CI), 0, RB), jax.random.fold_in(keys[7], 1), 0, RB - 1).astype(jnp.int32)
    send_far = place_ends(jax.random.randint(keys[8], (DEVICES, DEVICES, CC), 0, RB), jax.random.fold_in(keys[8], 1), 0, RB - 1).astype(jnp.int32)
    return dict(vec_x=vec_x, vec_p=vec_p, diag_shift=diag_shift, tiles=tiles, tile_row=tile_row, tile_col=tile_col, tile_count=tile_count, send_near=send_near, send_far=send_far)


exact_mode = lax.Precision.HIGHEST

def degree_of(diag_shift, tiles, tile_row, tile_count):
    tiles_dev = tiles.reshape(DEVICES, NT, BLK, BLK)
    rows_dev = tile_row.reshape(DEVICES, NT)

    def one_device(packed):
        tile_set, row_set, live = packed
        totals = lax.optimization_barrier(jnp.sum(tile_set.astype(jnp.float32), axis=2))
        living = (jnp.arange(NT, dtype=jnp.int32) < live).astype(totals.dtype)
        return jax.ops.segment_sum(totals * living[:, None], row_set, num_segments=RB)
    per_device = lax.map(one_device, (tiles_dev, rows_dev, tile_count))
    return per_device.reshape(DEVICES * RB * BLK) + diag_shift

def operate(field, degree, tiles, tile_row, tile_col, tile_count, send_near, send_far):
    width = field.shape[0]
    blocks_all = field.reshape(width, DEVICES, RB, BLK)
    tiles_dev = tiles.reshape(DEVICES, NT, BLK, BLK)
    rows_dev = tile_row.reshape(DEVICES, NT)
    cols_dev = tile_col.reshape(DEVICES, NT)
    degree_dev = degree.reshape(DEVICES, RB * BLK)

    def one_device(packed):
        device, tile_set, row_set, col_set, live, diag_part = packed
        community = device // N_INNER
        position = device % N_INNER
        peers = community * N_INNER + jnp.arange(N_INNER, dtype=jnp.int32)
        near_index = send_near[peers, position]
        near_blocks = blocks_all[:, peers[:, None], near_index]
        far_index = send_far[:, device]
        far_blocks = blocks_all[:, jnp.arange(DEVICES, dtype=jnp.int32)[:, None], far_index]
        own_blocks = blocks_all[:, device]
        pooled = jnp.concatenate([own_blocks, near_blocks.reshape(width, -1, BLK), far_blocks.reshape(width, -1, BLK)], axis=1)
        picked = pooled[:, col_set]
        contrib = jnp.einsum('knc,nrc->nkr', picked.astype(jnp.float32), tile_set.astype(jnp.float32))
        living = (jnp.arange(NT, dtype=jnp.int32) < live).astype(contrib.dtype)
        contrib = contrib * living[:, None, None]
        summed = jax.ops.segment_sum(contrib, row_set, num_segments=RB)
        summed = jnp.transpose(summed, (1, 0, 2)).reshape(width, RB * BLK)
        return diag_part[None, :] * own_blocks.astype(jnp.float32).reshape(width, RB * BLK) - summed
    outputs = lax.map(one_device, (jnp.arange(DEVICES, dtype=jnp.int32), tiles_dev, rows_dev, cols_dev, tile_count, degree_dev))
    return jnp.transpose(outputs, (1, 0, 2)).reshape(width, DEVICES * RB * BLK)

def ritz_solve(gram, proj, width):
    basis_len = gram.shape[0]
    symmetric = 0.5 * (proj + proj.T)
    factor = jnp.linalg.cholesky(gram)
    halfway = jax.scipy.linalg.solve_triangular(factor, symmetric, lower=True)
    reduced = jax.scipy.linalg.solve_triangular(factor, halfway.T, lower=True)
    reduced = 0.5 * (reduced + reduced.T)
    identity_mat = jnp.eye(basis_len, dtype=jnp.float32)
    center = jnp.trace(reduced) / basis_len
    moved = reduced - center * identity_mat
    signum = moved / jnp.sqrt(jnp.sum(moved * moved) + 1e-06)
    for repeat in range(NS):
        square = jnp.dot(signum, signum, precision=exact_mode)
        signum = 1.5 * signum - 0.5 * jnp.dot(square, signum, precision=exact_mode)
    low_proj = 0.5 * (identity_mat - signum)
    target = jnp.dot(low_proj, factor[:width, :].T, precision=exact_mode)
    return jax.scipy.linalg.solve_triangular(factor, target, lower=True, trans=1)

def reference(vec_x, vec_p, diag_shift, tiles, tile_row, tile_col, tile_count, send_near, send_far):
    width = vec_x.shape[0]
    degree = degree_of(diag_shift, tiles, tile_row, tile_count)
    extras = (tiles, tile_row, tile_col, tile_count, send_near, send_far)
    both = jnp.concatenate([vec_x, vec_p], axis=0)
    image = operate(both, degree, *extras)
    image_x = image[:width]
    x_wide = vec_x.astype(jnp.float32)
    numer = lax.optimization_barrier(jnp.sum(x_wide * image_x, axis=1))
    denom = lax.optimization_barrier(jnp.sum(x_wide * x_wide, axis=1))
    ratio = numer / (denom + 1e-06)
    search = ((image_x - ratio[:, None] * x_wide) / degree[None, :]).astype(jnp.bfloat16)
    image_w = operate(search, degree, *extras)
    basis = jnp.concatenate([vec_x, vec_p, search], axis=0)
    applied = jnp.concatenate([image, image_w], axis=0).astype(jnp.bfloat16)
    gram = jnp.dot(basis.astype(jnp.float32), basis.T.astype(jnp.float32), preferred_element_type=jnp.float32)
    proj = jnp.dot(basis.astype(jnp.float32), applied.T.astype(jnp.float32), preferred_element_type=jnp.float32)
    coeff = ritz_solve(gram, proj, width).astype(jnp.bfloat16)
    next_x = jnp.dot(coeff.T.astype(jnp.float32), basis.astype(jnp.float32), preferred_element_type=jnp.float32)
    next_p = jnp.dot(coeff[width:].T.astype(jnp.float32), basis[width:].astype(jnp.float32), preferred_element_type=jnp.float32)
    return (next_x, next_p)
```

```python
import functools
import math

import jax
import jax.numpy as jnp
from jax import lax
from jax.experimental import pallas as pl
from jax.experimental.pallas import tpu as pltpu
from jax.sharding import PartitionSpec as P

NS = 6
CHUNK = 8
BOTH = ("comm", "inner")
MIB = 1 << 20
exact_mode = lax.Precision.HIGHEST
f32, bf16 = jnp.float32, jnp.bfloat16
NT_DIMS = (((1,), (1,)), ((), ()))
VMEM = pl.BlockSpec(memory_space=pltpu.VMEM)
SMEM = pl.BlockSpec(memory_space=pltpu.SMEM)
HBM = pl.BlockSpec(memory_space=pl.ANY)


def nt_dot(a, b):
    return lax.dot_general(a, b, NT_DIMS, preferred_element_type=f32)


def exact_dot(a, b):
    return jnp.dot(a, b, precision=exact_mode, preferred_element_type=f32)


def cost(flops, nbytes):
    return pl.CostEstimate(flops=int(flops), bytes_accessed=int(nbytes), transcendentals=0)


def pack_kernel(per, index_ref, blocks_ref, out_ref):
    step = pl.program_id(0)
    for e in range(per):
        out_ref[e] = blocks_ref[index_ref[step * per + e]]


def pack(index, blocks, per=16):
    count = index.shape[0]
    _, width, size = blocks.shape
    return pl.pallas_call(
        functools.partial(pack_kernel, per),
        grid_spec=pltpu.PrefetchScalarGridSpec(
            num_scalar_prefetch=1,
            grid=(count // per,),
            in_specs=[pl.BlockSpec(blocks.shape, lambda g, s: (0, 0, 0))],
            out_specs=pl.BlockSpec((per, width, size), lambda g, s: (g, 0, 0)),
        ),
        out_shape=jax.ShapeDtypeStruct((count, width, size), blocks.dtype),
        compiler_params=pltpu.CompilerParams(vmem_limit_bytes=32 * MIB),
        cost_estimate=cost(0, 2 * count * width * size * 2),
        name="pack",
    )(index, blocks)


def degree_kernel(row_ref, count_ref, tile_ref, shift_ref, out_ref, acc):
    step = pl.program_id(0)
    own = shift_ref.shape[0]

    @pl.when(step == 0)
    def _():
        acc[...] = jnp.zeros_like(acc)

    ones = jnp.ones((16, tile_ref.shape[2]), bf16)
    for e in range(CHUNK):
        t = step * CHUNK + e
        row = jnp.where(t < count_ref[0], row_ref[t], own)
        acc[row] = acc[row] + nt_dot(ones, tile_ref[e])[:8]

    @pl.when(step == pl.num_programs(0) - 1)
    def _():
        for b in range(own):
            out_ref[b : b + 1, :] = acc[b, 0:1, :] + shift_ref[b : b + 1, :]


def degree_of(tiles, tile_row, tile_count, shift):
    slots, size, _ = tiles.shape
    own = shift.shape[0]
    return pl.pallas_call(
        degree_kernel,
        grid_spec=pltpu.PrefetchScalarGridSpec(
            num_scalar_prefetch=2,
            grid=(slots // CHUNK,),
            in_specs=[
                pl.BlockSpec((CHUNK, size, size), lambda g, r, c: (g, 0, 0)),
                pl.BlockSpec(shift.shape, lambda g, r, c: (0, 0)),
            ],
            out_specs=pl.BlockSpec(shift.shape, lambda g, r, c: (0, 0)),
            scratch_shapes=[pltpu.VMEM((own + 1, 8, size), f32)],
        ),
        out_shape=jax.ShapeDtypeStruct(shift.shape, f32),
        compiler_params=pltpu.CompilerParams(vmem_limit_bytes=32 * MIB),
        cost_estimate=cost(2 * 16 * slots * size * size, slots * size * size * 2),
        name="degree",
    )(tile_row, tile_count, tiles, shift)


def tile_sums(step, row_ref, col_ref, count_ref, table_ref, tile_ref, near_ref, far_ref, pool, acc, sems):
    own = acc.shape[0] - 1
    near = near_ref.shape[0]

    @pl.when(step == 0)
    def _():
        first = pltpu.make_async_copy(near_ref, pool.at[pl.ds(0, near)], sems.at[0])
        second = pltpu.make_async_copy(far_ref, pool.at[pl.ds(near, far_ref.shape[0])], sems.at[1])
        first.start()
        second.start()
        acc[...] = jnp.zeros_like(acc)
        first.wait()
        second.wait()

    for e in range(CHUNK):
        t = step * CHUNK + e
        row = jnp.where(t < count_ref[0], row_ref[t], own)
        picked = pool[table_ref[col_ref[t]]]
        acc[row] = acc[row] + nt_dot(picked, tile_ref[e])


def first_kernel(width, row_ref, col_ref, count_ref, table_ref, tile_ref, near_ref, far_ref, degree_ref,
                 image_ref, low_ref, gram_ref, ratio_ref, pool, acc, sems):
    step = pl.program_id(0)
    own = degree_ref.shape[0]
    tile_sums(step, row_ref, col_ref, count_ref, table_ref, tile_ref, near_ref, far_ref, pool, acc, sems)

    @pl.when(step == pl.num_programs(0) - 1)
    def _():
        start = table_ref[0]
        numer = denom = gram = proj = 0.0
        for b in range(own):
            field = pool[start + b]
            wide = field.astype(f32)
            image = degree_ref[b : b + 1, :] * wide - acc[b]
            low = image.astype(bf16)
            image_ref[b] = image[:width]
            low_ref[b] = low
            numer = numer + wide[:width] * image[:width]
            denom = denom + wide[:width] * wide[:width]
            gram = gram + nt_dot(field, field)
            proj = proj + nt_dot(field, low)
        gram_ref[0] = gram
        gram_ref[1] = proj
        ratio_ref[0] = numer
        ratio_ref[1] = denom


def second_kernel(row_ref, col_ref, count_ref, table_ref, tile_ref, near_ref, far_ref, degree_ref, blocks_ref,
                  proj_ref, pool, acc, sems):
    step = pl.program_id(0)
    own = degree_ref.shape[0]
    tile_sums(step, row_ref, col_ref, count_ref, table_ref, tile_ref, near_ref, far_ref, pool, acc, sems)

    @pl.when(step == pl.num_programs(0) - 1)
    def _():
        start = table_ref[0]
        first = last = 0.0
        for b in range(own):
            field = pool[start + b]
            low = (degree_ref[b : b + 1, :] * field.astype(f32) - acc[b]).astype(bf16)
            first = first + nt_dot(blocks_ref[b], low)
            last = last + nt_dot(field, low)
        proj_ref[0 : first.shape[0]] = first
        proj_ref[first.shape[0] :] = last


def apply_tiles(kernel, out_shape, plan, tiles, near, far, extra, name):
    slots, size, _ = tiles.shape
    width = near.shape[1]
    own = extra[0].shape[0]
    whole = lambda a: pl.BlockSpec(a.shape, lambda g, *_: (0,) * len(a.shape))
    return pl.pallas_call(
        kernel,
        grid_spec=pltpu.PrefetchScalarGridSpec(
            num_scalar_prefetch=4,
            grid=(slots // CHUNK,),
            in_specs=[pl.BlockSpec((CHUNK, size, size), lambda g, *_: (g, 0, 0)), HBM, HBM]
            + [whole(a) for a in extra],
            out_specs=[whole(a) for a in out_shape],
            scratch_shapes=[
                pltpu.VMEM((near.shape[0] + far.shape[0], width, size), bf16),
                pltpu.VMEM((own + 1, width, size), f32),
                pltpu.SemaphoreType.DMA((2,)),
            ],
        ),
        out_shape=out_shape,
        compiler_params=pltpu.CompilerParams(vmem_limit_bytes=48 * MIB),
        cost_estimate=cost(2 * width * slots * size * size, slots * size * size * 2 + 2 * near.size * 2),
        name=name,
    )(*plan, tiles, near, far, *extra)


def search_kernel(ratio_ref, image_ref, blocks_ref, degree_ref, out_ref):
    width = image_ref.shape[1]
    ratio = ratio_ref[...]
    for b in range(image_ref.shape[0]):
        x = blocks_ref[b][:width].astype(f32)
        out_ref[b] = ((image_ref[b] - ratio * x) / degree_ref[b : b + 1, :]).astype(bf16)


def search_of(ratio, image_x, blocks, degree):
    return pl.pallas_call(
        search_kernel,
        in_specs=[VMEM] * 4,
        out_specs=VMEM,
        out_shape=jax.ShapeDtypeStruct(image_x.shape, bf16),
        cost_estimate=cost(0, image_x.size * 8),
        name="search",
    )(ratio, image_x, blocks, degree)


def cross_kernel(blocks_ref, search_ref, low_ref, out_ref):
    upper = lower = proj = 0.0
    for b in range(blocks_ref.shape[0]):
        s = search_ref[b]
        upper = upper + nt_dot(blocks_ref[b], s)
        lower = lower + nt_dot(s, s)
        proj = proj + nt_dot(low_ref[b], s)
    n, m = upper.shape
    out_ref[0, 0:n] = upper
    out_ref[0, n : n + m] = lower
    out_ref[1, 0:n] = proj
    out_ref[1, n : n + m] = jnp.zeros_like(lower)


def cross_of(blocks, search, low):
    n, m = blocks.shape[1], search.shape[1]
    return pl.pallas_call(
        cross_kernel,
        in_specs=[VMEM] * 3,
        out_specs=VMEM,
        out_shape=jax.ShapeDtypeStruct((2, n + m, m), f32),
        cost_estimate=cost(2 * 16 * 96 * 256 * 96, blocks.size * 6),
        name="cross",
    )(blocks, search, low)


def ritz_kernel(width, gram_ref, proj_ref, blocks_ref, search_ref, x_ref, p_ref):
    n = gram_ref.shape[0]
    rows = lax.broadcasted_iota(jnp.int32, (n, n), 0)
    cols = lax.broadcasted_iota(jnp.int32, (n, n), 1)
    eye = (rows == cols).astype(f32)
    a = gram_ref[...]
    for k in range(n):
        inv = 1.0 / a[k : k + 1, k : k + 1]
        line = a[k : k + 1, :]
        side = a[:, k : k + 1] * inv
        scaled = line * inv
        new = a - side * line
        new = jnp.where(rows == k, scaled, new)
        new = jnp.where(cols == k, side, new)
        a = jnp.where((rows == k) & (cols == k), -inv, new)
    proj = proj_ref[...]
    sym = 0.5 * (proj + proj.T)
    reduced = -exact_dot(a, sym)
    center = jnp.sum(reduced * eye) / n
    moved = reduced - center * eye
    signum = moved * lax.rsqrt(jnp.sum(moved * moved.T) + 1e-06)
    for _ in range(NS):
        square = exact_dot(signum, signum)
        signum = 1.5 * signum - 0.5 * exact_dot(square, signum)
    low_proj = 0.5 * (eye - signum)
    coeff = low_proj.T[:width, :]
    lanes = lax.broadcasted_iota(jnp.int32, coeff.shape, 1)
    both = jnp.concatenate([coeff, jnp.where(lanes < width, 0.0, coeff)], axis=0).astype(bf16)
    m = blocks_ref.shape[1]
    size = blocks_ref.shape[2]
    for b in range(blocks_ref.shape[0]):
        basis = jnp.concatenate([blocks_ref[b], search_ref[b]], axis=0)
        out = jnp.dot(both, basis, preferred_element_type=f32)
        x_ref[:, b * size : (b + 1) * size] = out[:width]
        p_ref[:, b * size : (b + 1) * size] = out[width:]


def ritz(gram, proj, blocks, search):
    own, width, size = search.shape
    shape = jax.ShapeDtypeStruct((width, own * size), f32)
    return pl.pallas_call(
        functools.partial(ritz_kernel, width),
        in_specs=[VMEM] * 4,
        out_specs=[VMEM] * 2,
        out_shape=[shape, shape],
        compiler_params=pltpu.CompilerParams(vmem_limit_bytes=32 * MIB),
        cost_estimate=cost(2 * 14 * 6 * 96**3, 2 * MIB),
        name="ritz",
    )(gram, proj, blocks, search)


def exchange(a, axes):
    return lax.all_to_all(a, axes, split_axis=0, concat_axis=0, tiled=True)


def spread(a, axis, count):
    return exchange(jnp.broadcast_to(a[None], (count,) + a.shape), axis)


def total(a, inner, comm):
    part = a.reshape(inner, -1, 128)
    part = jnp.sum(exchange(part, "inner"), axis=0)
    part = jnp.sum(spread(part, "comm", comm), axis=0)
    return spread(part, "inner", inner).reshape(a.shape)


def shards(inner, comm, vec_x, vec_p, diag_shift, tiles, tile_row, tile_col, tile_count, send_near, send_far):
    width = vec_x.shape[0]
    size = tiles.shape[1]
    own = diag_shift.shape[0] // size
    place = lax.axis_index("inner")
    blocks = jnp.concatenate([vec_x, vec_p], axis=0).reshape(2 * width, own, size).transpose(1, 0, 2)
    far_index = send_far.reshape(-1)
    near_sets = lax.all_gather(send_near.reshape(inner, -1), "inner", axis=0)
    near_mine = lax.dynamic_index_in_dim(near_sets, place, axis=1, keepdims=False)
    near_place = near_mine + own * jnp.arange(inner, dtype=jnp.int32)[:, None]
    table = jnp.concatenate([
        place * own + jnp.arange(own, dtype=jnp.int32),
        near_place.reshape(-1),
        inner * own + jnp.arange(far_index.shape[0], dtype=jnp.int32),
    ])
    plan = (tile_row, tile_col, tile_count, table)

    near = lax.all_gather(blocks, "inner", axis=0, tiled=True)
    far = exchange(pack(far_index, blocks), BOTH)
    degree = degree_of(tiles, tile_row, tile_count, diag_shift.reshape(own, size))
    image_x, low, gram_a, sums = apply_tiles(
        functools.partial(first_kernel, width),
        [
            jax.ShapeDtypeStruct((own, width, size), f32),
            jax.ShapeDtypeStruct((own, 2 * width, size), bf16),
            jax.ShapeDtypeStruct((2, 2 * width, 2 * width), f32),
            jax.ShapeDtypeStruct((2, width, size), f32),
        ],
        plan, tiles, near, far, [degree], "first",
    )
    sums = jnp.sum(sums, axis=2).reshape(1, 2 * width)
    sums = jnp.sum(spread(sums, BOTH, inner * comm), axis=(0, 1))
    ratio = (sums[:width] / (sums[width:] + 1e-06)).reshape(width, 1)
    search = search_of(ratio, image_x, blocks, degree)

    near = lax.all_gather(search, "inner", axis=0, tiled=True)
    far = exchange(pack(far_index, search), BOTH)
    cross = cross_of(blocks, search, low)
    (proj_w,) = apply_tiles(
        second_kernel, [jax.ShapeDtypeStruct((3 * width, width), f32)],
        plan, tiles, near, far, [degree, blocks], "second",
    )
    n = 2 * width
    packed = jnp.concatenate([gram_a.reshape(-1), cross.reshape(-1), proj_w.reshape(-1)])
    packed = total(packed, inner, comm)
    a, b, c = jnp.split(packed, [gram_a.size, gram_a.size + cross.size])
    gram_a, cross, proj_w = a.reshape(gram_a.shape), b.reshape(cross.shape), c.reshape(proj_w.shape)
    gram = jnp.concatenate([
        jnp.concatenate([gram_a[0], cross[0, :n]], axis=1),
        jnp.concatenate([cross[0, :n].T, cross[0, n:]], axis=1),
    ], axis=0)
    proj = jnp.concatenate([
        jnp.concatenate([gram_a[1], cross[1, :n].T], axis=0), proj_w], axis=1)
    return tuple(ritz(gram, proj, blocks, search))


def solution(mesh):
    in_specs = (
        P(None, BOTH),
        P(None, BOTH),
        P(BOTH),
        P(BOTH, None, None),
        P(BOTH),
        P(BOTH),
        P(BOTH),
        P(BOTH, None, None),
        P(BOTH, None, None),
    )
    out_specs = (P(None, BOTH), P(None, BOTH))
    run = functools.partial(shards, mesh.shape["inner"], mesh.shape["comm"])
    return jax.shard_map(run, mesh=mesh, in_specs=in_specs, out_specs=out_specs, check_vma=False)
```

```python
import functools

import jax
import jax.numpy as jnp
from jax import lax
from jax.experimental import pallas as pl
from jax.experimental.pallas import tpu as pltpu
from jax.sharding import PartitionSpec as P

NS = 6
CHUNK = 24
AHEAD = 2
LIMIT = 60
BOTH = ("comm", "inner")
MIB = 1 << 20
exact_mode = lax.Precision.HIGHEST
f32, bf16, i32 = jnp.float32, jnp.bfloat16, jnp.int32
NT_DIMS = (((1,), (1,)), ((), ()))
VMEM = pl.BlockSpec(memory_space=pltpu.VMEM)
SMEM = pl.BlockSpec(memory_space=pltpu.SMEM)
HBM = pl.BlockSpec(memory_space=pltpu.HBM)


def nt_dot(a, b):
    return lax.dot_general(a, b, NT_DIMS, preferred_element_type=f32)


def exact_dot(a, b):
    return jnp.dot(a, b, precision=exact_mode, preferred_element_type=f32)


def cost(flops, nbytes):
    return pl.CostEstimate(flops=int(flops), bytes_accessed=int(nbytes), transcendentals=0)


def call(kernel, name, specs, out_shape, scratch, flops, nbytes, limit=LIMIT):
    whole = lambda a: pl.BlockSpec(a.shape, lambda g: (0,) * len(a.shape))
    return pl.pallas_call(
        kernel,
        grid=(1,),
        in_specs=[whole(s) if isinstance(s, (jax.Array, jax.core.Tracer)) else s for s in specs],
        out_specs=[whole(a) for a in out_shape],
        out_shape=out_shape,
        scratch_shapes=scratch,
        compiler_params=pltpu.CompilerParams(vmem_limit_bytes=limit * MIB),
        cost_estimate=cost(flops, nbytes),
        name=name,
    )


def stream(tile_ref, held, sems, use):
    slots = sems.shape[0]
    steps = tile_ref.shape[0] // CHUNK
    copy = lambda k: pltpu.make_async_copy(
        tile_ref.at[pl.ds(k * CHUNK, CHUNK)], held.at[pl.ds(k % slots * CHUNK, CHUNK)], sems.at[k % slots])

    @pl.loop(0, steps)
    def _(k):
        copy(k).wait()

        @pl.when(k + AHEAD < steps)
        def _():
            copy(k + AHEAD).start()

        for e in range(CHUNK):
            use(k * CHUNK + e, held.at[k % slots * CHUNK + e])


def stream_start(tile_ref, held, sems):
    for k in range(AHEAD):
        pltpu.make_async_copy(
            tile_ref.at[pl.ds(k * CHUNK, CHUNK)], held.at[pl.ds(k * CHUNK, CHUNK)], sems.at[k]).start()


def stream_scratch(size):
    return [pltpu.VMEM(((AHEAD + 1) * CHUNK, size, size), bf16), pltpu.SemaphoreType.DMA((AHEAD + 1,))]


def degree_kernel(row_ref, count_ref, tile_ref, shift_ref, out_ref, acc, held, sems):
    own, size = shift_ref.shape
    stream_start(tile_ref, held, sems)
    acc[...] = jnp.zeros_like(acc)
    ones = jnp.ones((16, size), bf16)

    def use(t, tile):
        row = jnp.where(t < count_ref[0], row_ref[t], own)
        acc[row] = acc[row] + nt_dot(ones, tile[...])[:8]

    stream(tile_ref, held, sems, use)
    for b in range(own):
        out_ref[b : b + 1, :] = acc[b, 0:1, :] + shift_ref[b : b + 1, :]


def degree_of(tiles, tile_row, tile_count, shift):
    size = tiles.shape[1]
    return call(
        degree_kernel, "degree", [SMEM, SMEM, HBM, shift], [jax.ShapeDtypeStruct(shift.shape, f32)],
        [pltpu.VMEM((shift.shape[0] + 1, 8, size), f32)] + stream_scratch(size), 1.2e10, tiles.size,
    )(tile_row, tile_count, tiles, shift)[0]


def cut_kernel(own, far_index, near_index, place_ref, field_ref, *outs):
    blocks_ref = outs[0]
    size = blocks_ref.shape[2]
    for b in range(own):
        blocks_ref[b] = field_ref[:, b * size : (b + 1) * size]
    nears = outs[1:8]
    pick = nears[0].shape[0]
    for d, near_ref in enumerate(nears, 1):
        mate = (place_ref[0] + d) % (len(nears) + 1)
        for e in range(pick):
            near_ref[e] = blocks_ref[near_index[mate, e]]
    for far_ref in outs[8:]:
        for e in range(far_ref.shape[0]):
            far_ref[e] = blocks_ref[far_index[e]]


def cut(name, own, far_index, near_index, place, field, far):
    width, size = field.shape[0], field.shape[1] // own
    pick = near_index.shape[1]
    shape = lambda n: jax.ShapeDtypeStruct((n, width, size), bf16)
    out = [shape(own)] + [shape(pick)] * 7 + [shape(far_index.shape[0])] * far
    return call(
        functools.partial(cut_kernel, own), name, [SMEM] * 3 + [field], out, [], 0, 8 * field.size,
    )(far_index, near_index, place, field)


def tile_sums(plan, tile_ref, pool, acc, held, sems):
    row_ref, col_ref, count_ref, table_ref = plan
    own = acc.shape[0] - 1

    def use(t, tile):
        row = jnp.where(t < count_ref[0], row_ref[t], own)
        acc[row] = acc[row] + nt_dot(pool[table_ref[col_ref[t]]], tile[...])

    stream(tile_ref, held, sems, use)


def copy_all(pairs, sems):
    copies = [pltpu.make_async_copy(a, b, sems.at[k]) for k, (a, b) in enumerate(pairs)]
    for copy in copies:
        copy.start()
    return copies


def split3(a):
    high = a.astype(bf16)
    rest = a - high.astype(f32)
    mid = rest.astype(bf16)
    return high, mid, (rest - mid.astype(f32)).astype(bf16)


def row_sums(a):
    n = a.shape[0]
    turn = lax.broadcasted_iota(i32, (n, n), 0) == lax.broadcasted_iota(i32, (n, n), 1)
    column = jnp.broadcast_to(jnp.sum(a, axis=1, keepdims=True), (n, n))
    return jnp.sum(jnp.where(turn, column, 0.0), axis=0, keepdims=True)


def first_kernel(*refs):
    plan, far_index, near_index, place_ref = refs[:4], refs[4], refs[5], refs[6]
    tile_ref, own_ref, near_refs, far_ref = refs[7], refs[8], refs[9:16], refs[16]
    degree_ref, p_ref = refs[17:19]
    image_ref, low_ref, send_ref, around_refs = refs[19], refs[20], refs[21], refs[22:29]
    pool, acc, held, sems, pool_sems, ext = refs[29:]
    own, width = own_ref.shape[0], own_ref.shape[1]
    pick = near_refs[0].shape[0]
    pairs = [(own_ref, pool.at[pl.ds(0, own)])]
    pairs += [(ref, pool.at[pl.ds(own + k * pick, pick)]) for k, ref in enumerate(near_refs)]
    pairs += [(far_ref, pool.at[pl.ds(own + 7 * pick, far_ref.shape[0])])]
    copies = copy_all(pairs, pool_sems)
    stream_start(tile_ref, held, sems)
    acc[...] = jnp.zeros_like(acc)
    for copy in copies:
        copy.wait()
    tile_sums(plan, tile_ref, pool, acc, held, sems)
    numer = denom = 0.0
    for b in range(own):
        wide = pool[b].astype(f32)
        image = degree_ref[b : b + 1, :] * wide - acc[b]
        low = image.astype(bf16)
        image_ref[b] = image
        low_ref[b] = low
        ext[b, 0:width] = p_ref[b]
        ext[b, width : 2 * width] = low
        numer = numer + wide * image
        denom = denom + wide * wide
    terms = [jnp.concatenate([u, v], axis=1) for u, v in zip(split3(row_sums(numer)), split3(row_sums(denom)))]
    sums = jnp.concatenate(terms + [jnp.zeros_like(terms[0])], axis=1).astype(f32)
    at = lax.broadcasted_iota(i32, (8, sums.shape[1]), 0)
    for b in range(own):
        degree = degree_ref[b : b + 1, :]
        high = degree.astype(bf16).astype(f32)
        tail = jnp.where(at == 0, high, jnp.where(at == 1, degree - high, jnp.where(at == 2, sums, 0.0)))
        ext[b, 2 * width :] = tail.astype(bf16)
    for e in range(send_ref.shape[0]):
        send_ref[e] = ext[far_index[e]]
    for d, ref in enumerate(around_refs, 1):
        mate = (place_ref[0] + d) % 8
        for e in range(pick):
            ref[e] = ext[near_index[mate, e], width:]


def op_x(plan, far_index, near_index, place, tiles, own_x, nears, far, degree, p):
    own, width, size = own_x.shape
    pick = nears[0].shape[0]
    blocks = own + 7 * pick + far.shape[0]
    out = [
        jax.ShapeDtypeStruct(own_x.shape, f32),
        jax.ShapeDtypeStruct(own_x.shape, bf16),
        jax.ShapeDtypeStruct((far.shape[0], 2 * width + 8, size), bf16),
    ] + [jax.ShapeDtypeStruct((pick, width + 8, size), bf16)] * 7
    return call(
        first_kernel, "op_x", [SMEM] * 7 + [HBM] * 10 + [degree, p], out,
        [pltpu.VMEM((blocks, width, size), bf16), pltpu.VMEM((own + 1, width, size), f32)] + stream_scratch(size)
        + [pltpu.SemaphoreType.DMA((9,)), pltpu.VMEM((own, 2 * width + 8, size), bf16)],
        1.2e10, tiles.size,
    )(*plan, far_index, near_index, place, tiles, own_x, *nears, far, degree, p)


def last_kernel(*refs):
    plan, tile_ref = refs[:4], refs[4]
    near_x, near_p, near_low = refs[5:12], refs[12:19], refs[19:26]
    far_x_ref, far_ref = refs[26:28]
    degree_ref, x_ref, p_ref, image_ref, low_x_ref = refs[28:33]
    search_ref, out_ref = refs[33:35]
    pool, acc, held, sems, pool_sems, xs, lows, fars = refs[35:]
    own, width, size = x_ref.shape
    pick = near_x[0].shape[0]
    near, far = 7 * pick, far_ref.shape[0]
    pairs = [(far_ref, fars), (far_x_ref, xs.at[pl.ds(near, far)])]
    for k in range(7):
        pairs.append((near_x[k], xs.at[pl.ds(k * pick, pick)]))
        pairs.append((near_low[k], lows.at[pl.ds(k * pick, pick)]))
        pairs.append((near_p[k], pool.at[pl.ds(own + k * pick, pick), pl.ds(0, width)]))
    copies = copy_all(pairs, pool_sems)
    stream_start(tile_ref, held, sems)
    acc[...] = jnp.zeros_like(acc)
    copies[0].wait()

    def add(k, total):
        for e in range(8):
            total = total + fars[k * 8 + e, 2 * width :].astype(f32)
        return total

    sums = lax.fori_loop(0, far // 8, add, jnp.zeros((8, size), f32))[2:3, :]
    two = 2 * width
    sums = sums[:, :two] + sums[:, two : 2 * two] + sums[:, 2 * two : 3 * two]
    ratio = sums[:, :width] / (sums[:, width:two] + 1e-06)
    square = (width, width)
    turn = lax.broadcasted_iota(i32, square, 0) == lax.broadcasted_iota(i32, square, 1)
    ratio = jnp.sum(jnp.where(turn, jnp.broadcast_to(ratio, square), 0.0), axis=1, keepdims=True)

    for b in range(own):
        s = ((image_ref[b] - ratio * x_ref[b].astype(f32)) / degree_ref[b : b + 1, :]).astype(bf16)
        search_ref[b] = s
        pool[b, 0:width] = p_ref[b]
        pool[b, width:] = s
    for copy in copies[1:]:
        copy.wait()

    def form(image, x, tail):
        tail = tail.astype(f32)
        inv = 1.0 / (tail[0:1] + tail[1:2])
        return ((image.astype(f32) - ratio * x.astype(f32)) * inv).astype(bf16)

    @pl.loop(0, 7)
    def _(k):
        for e in range(pick):
            m = k * pick + e
            pool[own + m, width:] = form(lows[m, 0:width], xs[m], lows[m, width:])

    @pl.loop(0, far // 8)
    def _(k):
        for e in range(8):
            m = k * 8 + e
            pool[own + near + m, 0:width] = fars[m, 0:width]
            pool[own + near + m, width:] = form(fars[m, width : 2 * width], xs[near + m], fars[m, 2 * width :])

    tile_sums(plan, tile_ref, pool, acc, held, sems)
    total = 0.0
    for b in range(own):
        field = pool[b]
        low = (degree_ref[b : b + 1, :] * field.astype(f32) - acc[b]).astype(bf16)
        basis = jnp.concatenate([x_ref[b], field], axis=0)
        total = total + nt_dot(basis, jnp.concatenate([basis, low_x_ref[b], low], axis=0))
    n = 3 * width
    rest = jnp.concatenate([total[: n // 2, 4 * width :], total[n // 2 :, 4 * width :]], axis=1)
    out_ref[:, 0, :] = jnp.concatenate([total[:, : 4 * width], rest], axis=0).T


def op_ps(plan, tiles, near_x, near_p, near_low, far_x, far, degree, x, p, image, low_x):
    own, width, size = x.shape
    pick = near_x[0].shape[0]
    near, count = 7 * pick, far.shape[0]
    n = 3 * width
    out = [jax.ShapeDtypeStruct(x.shape, bf16), jax.ShapeDtypeStruct((4 * width, 1, n + n // 2), f32)]
    return call(
        last_kernel, "op_ps", [SMEM] * 4 + [HBM] * 24 + [degree, x, p, image, low_x], out,
        [pltpu.VMEM((own + near + count, 2 * width, size), bf16), pltpu.VMEM((own + 1, 2 * width, size), f32)]
        + stream_scratch(size)
        + [
            pltpu.SemaphoreType.DMA((23,)),
            pltpu.VMEM((near + count, width, size), bf16),
            pltpu.VMEM((near, width + 8, size), bf16),
            pltpu.VMEM((count, 2 * width + 8, size), bf16),
        ],
        1.2e10, tiles.size,
    )(*plan, tiles, *near_x, *near_p, *near_low, far_x, far, degree, x, p, image, low_x)


def inverse(gram, eye, guess_ref, image_ref):
    root_row = lax.rsqrt(jnp.sum(gram * eye, axis=0, keepdims=True))
    root_col = lax.rsqrt(jnp.sum(gram * eye, axis=1, keepdims=True))
    scaled = gram * root_row * root_col
    bound = jnp.max(jnp.sum(jnp.abs(scaled), axis=1, keepdims=True))
    guess_ref[...] = eye / bound
    image_ref[...] = scaled / bound

    def improve(state):
        count, _ = state
        image = image_ref[...]
        guess = exact_dot(guess_ref[...], 2.0 * eye - image)
        guess_ref[...] = guess
        image_ref[...] = exact_dot(scaled, guess)
        return count + 1, jnp.max(jnp.abs(eye - image))

    lax.while_loop(lambda state: (state[1] > 3e-4) & (state[0] < 60), improve, (jnp.int32(0), jnp.float32(1.0)))
    return exact_dot(guess_ref[...], 2.0 * eye - image_ref[...]) * root_row * root_col


def ritz_kernel(sums_ref, x_ref, p_ref, s_ref, out_x_ref, out_p_ref, guess_ref, image_ref):
    width = x_ref.shape[1]
    n = 3 * width
    eye = (lax.broadcasted_iota(i32, (n, n), 0) == lax.broadcasted_iota(i32, (n, n), 1)).astype(f32)
    sums = sums_ref[:, 0, :].T
    late = sums[n:]
    late = jnp.concatenate([late[:, : 2 * width], late[:, 2 * width :]], axis=0)
    proj = jnp.concatenate([sums[0:n, n:], late], axis=1)
    sym = 0.5 * (proj + proj.T)
    reduced = exact_dot(inverse(sums[0:n, 0:n], eye, guess_ref, image_ref), sym)
    center = jnp.sum(reduced * eye) / n
    moved = reduced - center * eye
    signum = moved * lax.rsqrt(jnp.sum(moved * moved.T) + 1e-06)
    for _ in range(NS):
        square = exact_dot(signum, signum)
        signum = 1.5 * signum - 0.5 * exact_dot(square, signum)
    low_proj = 0.5 * (eye - signum)
    coeff = low_proj.T[:width, :]
    lanes = lax.broadcasted_iota(i32, coeff.shape, 1)
    both = jnp.concatenate([coeff, jnp.where(lanes < width, 0.0, coeff)], axis=0).astype(bf16)
    size = x_ref.shape[2]
    for b in range(out_x_ref.shape[1] // size):
        basis = jnp.concatenate([x_ref[b], p_ref[b], s_ref[b]], axis=0)
        out = jnp.dot(both, basis, preferred_element_type=f32)
        out_x_ref[:, b * size : (b + 1) * size] = out[:width]
        out_p_ref[:, b * size : (b + 1) * size] = out[width:]


def ritz(sums, x, p, search):
    own, width, size = p.shape
    shape = jax.ShapeDtypeStruct((width, own * size), f32)
    return call(
        ritz_kernel, "ritz", [sums, x, p, search], [shape, shape],
        [pltpu.VMEM((3 * width, 3 * width), f32)] * 2, 4e9, 2 * MIB,
    )(sums, x, p, search)


def exchange(a, axes):
    return lax.all_to_all(a, axes, split_axis=0, concat_axis=0, tiled=True)


def spread(a, axis, count):
    return exchange(jnp.broadcast_to(a[None], (count,) + a.shape), axis)


def total(a, devices):
    part = jnp.sum(exchange(a, BOTH), axis=0)
    return spread(part, BOTH, devices)


def pass_on(parts, inner):
    return [
        lax.ppermute(part, "inner", [(k, (k + d) % inner) for k in range(inner)])
        for d, part in enumerate(parts, 1)
    ]


def shards(inner, comm, vec_x, vec_p, diag_shift, tiles, tile_row, tile_col, tile_count, send_near, send_far):
    width = vec_x.shape[0]
    size = tiles.shape[1]
    own = diag_shift.shape[0] // size
    place = lax.axis_index("inner").astype(i32)
    devices = inner * comm
    pick = send_near.shape[2]
    far_index, near_index = send_far.reshape(-1), send_near[0]

    before = (place - jnp.arange(inner, dtype=i32)) % inner
    near_table = own + (before[:, None] - 1) * pick + jnp.arange(pick, dtype=i32)[None, :]
    mine = lax.dynamic_index_in_dim(send_near[0], place, axis=0, keepdims=True)
    near_table = jnp.where(before[:, None] == 0, mine, near_table)
    table = jnp.concatenate([
        jnp.arange(own, dtype=i32),
        near_table.reshape(-1),
        own + (inner - 1) * pick + jnp.arange(devices, dtype=i32),
    ])
    plan = (tile_row, tile_col, tile_count, table)
    spot = place.reshape(1)

    x, *rest = cut("cut_x", own, far_index, near_index, spot, vec_x, 1)
    far_x = exchange(rest[7], BOTH)
    near_x = pass_on(rest[:7], inner)
    degree = degree_of(tiles, tile_row, tile_count, diag_shift.reshape(own, size))
    p, *near_p = cut("cut_p", own, far_index, near_index, spot, vec_p, 0)
    far_x, p, near_p, degree = lax.optimization_barrier((far_x, p, near_p, degree))
    near_p = pass_on(near_p, inner)

    image, low_x, far, *near_low = op_x(
        plan, far_index, near_index, spot, tiles, x, near_x, far_x, degree, p)
    far, near_p = lax.optimization_barrier((far, near_p))
    far = exchange(far, BOTH)
    near_low = pass_on(near_low, inner)
    search, sums = op_ps(
        plan, tiles, near_x, near_p, near_low, far_x, far, degree, x, p, image, low_x)
    return tuple(ritz(total(sums, devices), x, p, search))


def solution(mesh):
    in_specs = (
        P(None, BOTH),
        P(None, BOTH),
        P(BOTH),
        P(BOTH, None, None),
        P(BOTH),
        P(BOTH),
        P(BOTH),
        P(BOTH, None, None),
        P(BOTH, None, None),
    )
    out_specs = (P(None, BOTH), P(None, BOTH))
    run = functools.partial(shards, mesh.shape["inner"], mesh.shape["comm"])
    return jax.shard_map(run, mesh=mesh, in_specs=in_specs, out_specs=out_specs, check_vma=False)
```

```python
import functools

import jax
import jax.numpy as jnp
from jax import lax
from jax.experimental import pallas as pl
from jax.experimental.pallas import tpu as pltpu
from jax.sharding import PartitionSpec as P

NS = 6
CHUNK = 24
AHEAD = 2
LIMIT = 60
BOTH = ("comm", "inner")
MIB = 1 << 20
exact_mode = lax.Precision.HIGHEST
f32, bf16, i32 = jnp.float32, jnp.bfloat16, jnp.int32
NT_DIMS = (((1,), (1,)), ((), ()))
VMEM = pl.BlockSpec(memory_space=pltpu.VMEM)
SMEM = pl.BlockSpec(memory_space=pltpu.SMEM)
HBM = pl.BlockSpec(memory_space=pltpu.HBM)


def nt_dot(a, b):
    return lax.dot_general(a, b, NT_DIMS, preferred_element_type=f32)


def exact_dot(a, b):
    return jnp.dot(a, b, precision=exact_mode, preferred_element_type=f32)


def cost(flops, nbytes):
    return pl.CostEstimate(flops=int(flops), bytes_accessed=int(nbytes), transcendentals=0)


def call(kernel, name, specs, out_shape, scratch, flops, nbytes, limit=LIMIT):
    whole = lambda a: pl.BlockSpec(a.shape, lambda g: (0,) * len(a.shape))
    return pl.pallas_call(
        kernel,
        grid=(1,),
        in_specs=[whole(s) if isinstance(s, (jax.Array, jax.core.Tracer)) else s for s in specs],
        out_specs=[whole(a) for a in out_shape],
        out_shape=out_shape,
        scratch_shapes=scratch,
        compiler_params=pltpu.CompilerParams(vmem_limit_bytes=limit * MIB),
        cost_estimate=cost(flops, nbytes),
        name=name,
    )


def stream(tile_ref, held, sems, use):
    slots = sems.shape[0]
    steps = tile_ref.shape[0] // CHUNK
    copy = lambda k: pltpu.make_async_copy(
        tile_ref.at[pl.ds(k * CHUNK, CHUNK)], held.at[pl.ds(k % slots * CHUNK, CHUNK)], sems.at[k % slots])

    @pl.loop(0, steps)
    def _(k):
        copy(k).wait()

        @pl.when(k + AHEAD < steps)
        def _():
            copy(k + AHEAD).start()

        for e in range(CHUNK):
            use(k * CHUNK + e, held.at[k % slots * CHUNK + e])


def stream_start(tile_ref, held, sems, first=0, last=AHEAD):
    for k in range(first, last):
        pltpu.make_async_copy(
            tile_ref.at[pl.ds(k * CHUNK, CHUNK)], held.at[pl.ds(k * CHUNK, CHUNK)], sems.at[k]).start()


def stream_scratch(size):
    return [pltpu.VMEM(((AHEAD + 1) * CHUNK, size, size), bf16), pltpu.SemaphoreType.DMA((AHEAD + 1,))]


def degree_kernel(row_ref, count_ref, tile_ref, shift_ref, out_ref, acc, held, sems):
    own, size = shift_ref.shape
    stream_start(tile_ref, held, sems)
    acc[...] = jnp.zeros_like(acc)
    ones = jnp.ones((16, size), bf16)

    def use(t, tile):
        row = jnp.where(t < count_ref[0], row_ref[t], own)
        acc[row] = acc[row] + nt_dot(ones, tile[...])[:8]

    stream(tile_ref, held, sems, use)
    for b in range(own):
        out_ref[b : b + 1, :] = acc[b, 0:1, :] + shift_ref[b : b + 1, :]


def degree_of(tiles, tile_row, tile_count, shift):
    size = tiles.shape[1]
    return call(
        degree_kernel, "degree", [SMEM, SMEM, HBM, shift], [jax.ShapeDtypeStruct(shift.shape, f32)],
        [pltpu.VMEM((shift.shape[0] + 1, 8, size), f32)] + stream_scratch(size), 1.2e10, tiles.size,
    )(tile_row, tile_count, tiles, shift)[0]


def cut_kernel(own, far_index, near_index, place_ref, field_ref, *outs):
    blocks_ref = outs[0]
    size = blocks_ref.shape[2]
    for b in range(own):
        blocks_ref[b] = field_ref[:, b * size : (b + 1) * size]
    nears = outs[1:8]
    pick = nears[0].shape[0]
    for d, near_ref in enumerate(nears, 1):
        mate = (place_ref[0] + d) % (len(nears) + 1)
        for e in range(pick):
            near_ref[e] = blocks_ref[near_index[mate, e]]
    for far_ref in outs[8:]:
        for e in range(far_ref.shape[0]):
            far_ref[e] = blocks_ref[far_index[e]]


def cut(name, own, far_index, near_index, place, field, far):
    width, size = field.shape[0], field.shape[1] // own
    pick = near_index.shape[1]
    shape = lambda n: jax.ShapeDtypeStruct((n, width, size), bf16)
    out = [shape(own)] + [shape(pick)] * 7 + [shape(far_index.shape[0])] * far
    return call(
        functools.partial(cut_kernel, own), name, [SMEM] * 3 + [field], out, [], 0, 8 * field.size,
    )(far_index, near_index, place, field)


def tile_sums(plan, tile_ref, pool, acc, held, sems):
    row_ref, col_ref, count_ref, table_ref = plan
    own = acc.shape[0] - 1

    def use(t, tile):
        row = jnp.where(t < count_ref[0], row_ref[t], own)
        acc[row] = acc[row] + nt_dot(pool[table_ref[col_ref[t]]], tile[...])

    stream(tile_ref, held, sems, use)


def copy_all(pairs, sems):
    copies = [pltpu.make_async_copy(a, b, sems.at[k]) for k, (a, b) in enumerate(pairs)]
    for copy in copies:
        copy.start()
    return copies


def split3(a):
    high = a.astype(bf16)
    rest = a - high.astype(f32)
    mid = rest.astype(bf16)
    return high, mid, (rest - mid.astype(f32)).astype(bf16)


def row_sums(a):
    n = a.shape[0]
    turn = lax.broadcasted_iota(i32, (n, n), 0) == lax.broadcasted_iota(i32, (n, n), 1)
    column = jnp.broadcast_to(jnp.sum(a, axis=1, keepdims=True), (n, n))
    return jnp.sum(jnp.where(turn, column, 0.0), axis=0, keepdims=True)


def first_kernel(*refs):
    plan, far_index, near_index, place_ref = refs[:4], refs[4], refs[5], refs[6]
    tile_ref, own_ref, near_refs, far_ref = refs[7], refs[8], refs[9:16], refs[16]
    degree_ref, p_ref = refs[17:19]
    image_ref, low_ref, send_ref, around_refs = refs[19], refs[20], refs[21], refs[22:29]
    pool, acc, held, sems, pool_sems, ext = refs[29:]
    own, width = own_ref.shape[0], own_ref.shape[1]
    pick = near_refs[0].shape[0]
    pairs = [(own_ref, pool.at[pl.ds(0, own)])]
    pairs += [(ref, pool.at[pl.ds(own + k * pick, pick)]) for k, ref in enumerate(near_refs)]
    pairs += [(far_ref, pool.at[pl.ds(own + 7 * pick, far_ref.shape[0])])]
    copies = copy_all(pairs, pool_sems)
    stream_start(tile_ref, held, sems, 0, 1)
    acc[...] = jnp.zeros_like(acc)
    for copy in copies:
        copy.wait()
    stream_start(tile_ref, held, sems, 1)
    tile_sums(plan, tile_ref, pool, acc, held, sems)
    half = degree_ref.shape[1] // 2
    numer = denom = 0.0
    for b in range(own):
        wide = pool[b].astype(f32)
        image = degree_ref[b : b + 1, :] * wide - acc[b]
        low = image.astype(bf16)
        image_ref[b] = image
        low_ref[b] = low
        for k, part in enumerate((p_ref[b][:, :half], low[:, :half], p_ref[b][:, half:], low[:, half:])):
            ext[b, k * width : (k + 1) * width] = part
        numer = numer + wide * image
        denom = denom + wide * wide
    terms = [jnp.concatenate([u, v], axis=1) for u, v in zip(split3(row_sums(numer)), split3(row_sums(denom)))]
    wide_sums = jnp.concatenate(terms + [jnp.zeros_like(terms[0])], axis=1).astype(f32)
    at = lax.broadcasted_iota(i32, (8, half), 0)
    for b in range(own):
        degree = degree_ref[b : b + 1, :]
        high = degree.astype(bf16).astype(f32)
        tail = jnp.zeros((8, half), f32)
        for k, row in enumerate((high, degree - high, wide_sums)):
            tail = jnp.where(at == 2 * k, row[:, :half], jnp.where(at == 2 * k + 1, row[:, half:], tail))
        ext[b, 4 * width :] = tail.astype(bf16)
    for e in range(send_ref.shape[0]):
        send_ref[e] = ext[far_index[e]]
    for d, ref in enumerate(around_refs, 1):
        mate = (place_ref[0] + d) % 8
        for e in range(pick):
            ref[e] = ext[near_index[mate, e]]


def op_x(plan, far_index, near_index, place, tiles, own_x, nears, far, degree, p):
    own, width, size = own_x.shape
    pick = nears[0].shape[0]
    blocks = own + 7 * pick + far.shape[0]
    out = [
        jax.ShapeDtypeStruct(own_x.shape, f32),
        jax.ShapeDtypeStruct(own_x.shape, bf16),
        jax.ShapeDtypeStruct((far.shape[0], 4 * width + 8, size // 2), bf16),
    ] + [jax.ShapeDtypeStruct((pick, 4 * width + 8, size // 2), bf16)] * 7
    return call(
        first_kernel, "op_x", [SMEM] * 7 + [HBM] * 10 + [degree, p], out,
        [pltpu.VMEM((blocks, width, size), bf16), pltpu.VMEM((own + 1, width, size), f32)] + stream_scratch(size)
        + [pltpu.SemaphoreType.DMA((9,)), pltpu.VMEM((own, 4 * width + 8, size // 2), bf16)],
        1.2e10, tiles.size,
    )(*plan, far_index, near_index, place, tiles, own_x, *nears, far, degree, p)


def last_kernel(*refs):
    plan, tile_ref = refs[:4], refs[4]
    near_x, near_refs, far_x_ref, far_ref = refs[5:12], refs[12:19], refs[19], refs[20]
    degree_ref, x_ref, p_ref, image_ref, low_x_ref = refs[21:26]
    search_ref, out_ref = refs[26:28]
    pool, acc, held, sems, pool_sems, xs, sent = refs[28:]
    own, width, size = x_ref.shape
    pick = near_x[0].shape[0]
    near, far = 7 * pick, far_ref.shape[0]
    pairs = [(far_ref, sent.at[pl.ds(near, far)]), (far_x_ref, xs.at[pl.ds(near, far)])]
    for k in range(7):
        pairs.append((near_x[k], xs.at[pl.ds(k * pick, pick)]))
        pairs.append((near_refs[k], sent.at[pl.ds(k * pick, pick)]))
    copies = copy_all(pairs, pool_sems)
    acc[...] = jnp.zeros_like(acc)
    copies[0].wait()
    stream_start(tile_ref, held, sems)

    def add(k, total):
        for e in range(8):
            total = total + sent[near + k * 8 + e, 4 * width :].astype(f32)
        return total

    sums = lax.fori_loop(0, far // 8, add, jnp.zeros((8, size // 2), f32))
    two = 2 * width
    sums = sums[4:5, :two] + sums[4:5, two:] + sums[5:6, :two]
    ratio = sums[:, :width] / (sums[:, width:two] + 1e-06)
    square = (width, width)
    turn = lax.broadcasted_iota(i32, square, 0) == lax.broadcasted_iota(i32, square, 1)
    ratio = jnp.sum(jnp.where(turn, jnp.broadcast_to(ratio, square), 0.0), axis=1, keepdims=True)

    for b in range(own):
        s = ((image_ref[b] - ratio * x_ref[b].astype(f32)) / degree_ref[b : b + 1, :]).astype(bf16)
        search_ref[b] = s
        pool[b, 0:width] = p_ref[b]
        pool[b, width:] = s
    for copy in copies[1:]:
        copy.wait()

    def join(left, right):
        return jnp.concatenate([left, right], axis=1)

    def form(image, x, tail):
        tail = tail.astype(f32)
        inv = 1.0 / (join(tail[0:1], tail[1:2]) + join(tail[2:3], tail[3:4]))
        return ((image.astype(f32) - ratio * x.astype(f32)) * inv).astype(bf16)

    @pl.loop(0, (near + far) // 8)
    def _(k):
        for e in range(8):
            m = k * 8 + e
            part = lambda r: join(sent[m, r * width : (r + 1) * width], sent[m, (r + 2) * width : (r + 3) * width])
            pool[own + m, 0:width] = part(0)
            pool[own + m, width:] = form(part(1), xs[m], sent[m, 4 * width :])

    tile_sums(plan, tile_ref, pool, acc, held, sems)
    total = 0.0
    for b in range(own):
        field = pool[b]
        low = (degree_ref[b : b + 1, :] * field.astype(f32) - acc[b]).astype(bf16)
        basis = jnp.concatenate([x_ref[b], field], axis=0)
        total = total + nt_dot(basis, jnp.concatenate([basis, low_x_ref[b], low], axis=0))
    n = 3 * width
    rest = jnp.concatenate([total[: n // 2, 4 * width :], total[n // 2 :, 4 * width :]], axis=1)
    out_ref[:, 0, :] = jnp.concatenate([total[:, : 4 * width], rest], axis=0).T


def op_ps(plan, tiles, near_x, near, far_x, far, degree, x, p, image, low_x):
    own, width, size = x.shape
    pick = near_x[0].shape[0]
    count = 7 * pick + far.shape[0]
    n = 3 * width
    out = [jax.ShapeDtypeStruct(x.shape, bf16), jax.ShapeDtypeStruct((4 * width, 1, n + n // 2), f32)]
    return call(
        last_kernel, "op_ps", [SMEM] * 4 + [HBM] * 17 + [degree, x, p, image, low_x], out,
        [pltpu.VMEM((own + count, 2 * width, size), bf16), pltpu.VMEM((own + 1, 2 * width, size), f32)]
        + stream_scratch(size)
        + [
            pltpu.SemaphoreType.DMA((16,)),
            pltpu.VMEM((count, width, size), bf16),
            pltpu.VMEM((count, 4 * width + 8, size // 2), bf16),
        ],
        1.2e10, tiles.size,
    )(*plan, tiles, *near_x, *near, far_x, far, degree, x, p, image, low_x)


def inverse(gram, eye, guess_ref, image_ref):
    root_row = lax.rsqrt(jnp.sum(gram * eye, axis=0, keepdims=True))
    root_col = lax.rsqrt(jnp.sum(gram * eye, axis=1, keepdims=True))
    scaled = gram * root_row * root_col
    bound = jnp.max(jnp.sum(jnp.abs(scaled), axis=1, keepdims=True))
    rough = scaled.astype(bf16)

    def improve(state):
        count, _ = state
        image = image_ref[...]
        guess = exact_dot(guess_ref[...], 2.0 * eye - image)
        guess_ref[...] = guess
        image_ref[...] = exact_dot(scaled, guess)
        return count + 1, jnp.max(jnp.abs(eye - image))

    start = (jnp.int32(0), jnp.float32(1.0))
    guess = eye / bound
    for _ in range(8):
        guess = guess.astype(bf16)
        image = jnp.dot(rough, guess, preferred_element_type=f32)
        guess = jnp.dot(guess, (2.0 * eye - image).astype(bf16), preferred_element_type=f32)
    guess_ref[...] = guess
    image_ref[...] = exact_dot(scaled, guess)
    away = jnp.max(jnp.sum(jnp.abs(eye - image_ref[...]), axis=1, keepdims=True))

    @pl.when(jnp.logical_not(away < 0.9))
    def _():
        guess_ref[...] = eye / bound
        image_ref[...] = scaled / bound

    lax.while_loop(lambda state: (state[1] > 3e-4) & (state[0] < 60), improve, start)
    return exact_dot(guess_ref[...], 2.0 * eye - image_ref[...]) * root_row * root_col


def ritz_kernel(sums_ref, x_ref, p_ref, s_ref, out_x_ref, out_p_ref, guess_ref, image_ref):
    width = x_ref.shape[1]
    n = 3 * width
    eye = (lax.broadcasted_iota(i32, (n, n), 0) == lax.broadcasted_iota(i32, (n, n), 1)).astype(f32)
    sums = sums_ref[:, 0, :].T
    late = sums[n:]
    late = jnp.concatenate([late[:, : 2 * width], late[:, 2 * width :]], axis=0)
    proj = jnp.concatenate([sums[0:n, n:], late], axis=1)
    sym = 0.5 * (proj + proj.T)
    reduced = exact_dot(inverse(sums[0:n, 0:n], eye, guess_ref, image_ref), sym)
    center = jnp.sum(reduced * eye) / n
    moved = reduced - center * eye
    signum = moved * lax.rsqrt(jnp.sum(moved * moved.T) + 1e-06)
    for _ in range(NS):
        square = exact_dot(signum, signum)
        signum = 1.5 * signum - 0.5 * exact_dot(square, signum)
    low_proj = 0.5 * (eye - signum)
    coeff = low_proj.T[:width, :]
    lanes = lax.broadcasted_iota(i32, coeff.shape, 1)
    both = jnp.concatenate([coeff, jnp.where(lanes < width, 0.0, coeff)], axis=0).astype(bf16)
    size = x_ref.shape[2]
    for b in range(out_x_ref.shape[1] // size):
        basis = jnp.concatenate([x_ref[b], p_ref[b], s_ref[b]], axis=0)
        out = jnp.dot(both, basis, preferred_element_type=f32)
        out_x_ref[:, b * size : (b + 1) * size] = out[:width]
        out_p_ref[:, b * size : (b + 1) * size] = out[width:]


def ritz(sums, x, p, search):
    own, width, size = p.shape
    shape = jax.ShapeDtypeStruct((width, own * size), f32)
    return call(
        ritz_kernel, "ritz", [sums, x, p, search], [shape, shape],
        [pltpu.VMEM((3 * width, 3 * width), f32)] * 2, 4e9, 2 * MIB,
    )(sums, x, p, search)


def exchange(a, axes):
    return lax.all_to_all(a, axes, split_axis=0, concat_axis=0, tiled=True)


def spread(a, axis, count):
    return exchange(jnp.broadcast_to(a[None], (count,) + a.shape), axis)


def total(a, devices):
    part = jnp.sum(exchange(a, BOTH), axis=0)
    return spread(part, BOTH, devices)


def pass_on(parts, inner):
    return [
        lax.ppermute(part, "inner", [(k, (k + d) % inner) for k in range(inner)])
        for d, part in enumerate(parts, 1)
    ]


def shards(inner, comm, vec_x, vec_p, diag_shift, tiles, tile_row, tile_col, tile_count, send_near, send_far):
    width = vec_x.shape[0]
    size = tiles.shape[1]
    own = diag_shift.shape[0] // size
    place = lax.axis_index("inner").astype(i32)
    devices = inner * comm
    pick = send_near.shape[2]
    far_index, near_index = send_far.reshape(-1), send_near[0]

    before = (place - jnp.arange(inner, dtype=i32)) % inner
    near_table = own + (before[:, None] - 1) * pick + jnp.arange(pick, dtype=i32)[None, :]
    mine = lax.dynamic_index_in_dim(send_near[0], place, axis=0, keepdims=True)
    near_table = jnp.where(before[:, None] == 0, mine, near_table)
    table = jnp.concatenate([
        jnp.arange(own, dtype=i32),
        near_table.reshape(-1),
        own + (inner - 1) * pick + jnp.arange(devices, dtype=i32),
    ])
    spot = place.reshape(1)

    x, *rest = cut("cut_x", own, far_index, near_index, spot, vec_x, 1)
    far_x = exchange(rest[7], BOTH)
    tile_row, table = lax.optimization_barrier((tile_row, table))
    plan = (tile_row, tile_col, tile_count, table)
    degree = degree_of(tiles, tile_row, tile_count, diag_shift.reshape(own, size))
    late, degree = lax.optimization_barrier((rest[4:7], degree))
    near_x = pass_on(rest[:4] + late, inner)
    p = vec_p.reshape(width, own, size).transpose(1, 0, 2)
    p, late = lax.optimization_barrier((p, late))

    image, low_x, far, *near = op_x(
        plan, far_index, near_index, spot, tiles, x, near_x, far_x, degree, p)
    far = exchange(far, BOTH)
    near = pass_on(near, inner)
    search, sums = op_ps(plan, tiles, near_x, near, far_x, far, degree, x, p, image, low_x)
    return tuple(ritz(total(sums, devices), x, p, search))


def solution(mesh):
    in_specs = (
        P(None, BOTH),
        P(None, BOTH),
        P(BOTH),
        P(BOTH, None, None),
        P(BOTH),
        P(BOTH),
        P(BOTH),
        P(BOTH, None, None),
        P(BOTH, None, None),
    )
    out_specs = (P(None, BOTH), P(None, BOTH))
    run = functools.partial(shards, mesh.shape["inner"], mesh.shape["comm"])
    return jax.shard_map(run, mesh=mesh, in_specs=in_specs, out_specs=out_specs, check_vma=False)
```

```python
import functools

import jax
import jax.numpy as jnp
from jax import lax
from jax.experimental import pallas as pl
from jax.experimental.pallas import tpu as pltpu
from jax.sharding import PartitionSpec as P

NS = 6
CHUNK = 24
AHEAD = 2
LIMIT = 60
BOTH = ("comm", "inner")
MIB = 1 << 20
exact_mode = lax.Precision.HIGHEST
f32, bf16, i32 = jnp.float32, jnp.bfloat16, jnp.int32
NT_DIMS = (((1,), (1,)), ((), ()))
VMEM = pl.BlockSpec(memory_space=pltpu.VMEM)
SMEM = pl.BlockSpec(memory_space=pltpu.SMEM)
HBM = pl.BlockSpec(memory_space=pltpu.HBM)


def nt_dot(a, b):
    return lax.dot_general(a, b, NT_DIMS, preferred_element_type=f32)


def exact_dot(a, b):
    return jnp.dot(a, b, precision=exact_mode, preferred_element_type=f32)


def cost(flops, nbytes):
    return pl.CostEstimate(flops=int(flops), bytes_accessed=int(nbytes), transcendentals=0)


def call(kernel, name, specs, out_shape, scratch, flops, nbytes, limit=LIMIT):
    whole = lambda a: pl.BlockSpec(a.shape, lambda g: (0,) * len(a.shape))
    return pl.pallas_call(
        kernel,
        grid=(1,),
        in_specs=[whole(s) if isinstance(s, (jax.Array, jax.core.Tracer)) else s for s in specs],
        out_specs=[whole(a) for a in out_shape],
        out_shape=out_shape,
        scratch_shapes=scratch,
        compiler_params=pltpu.CompilerParams(vmem_limit_bytes=limit * MIB),
        cost_estimate=cost(flops, nbytes),
        name=name,
    )


def stream(tile_ref, held, sems, use):
    slots = sems.shape[0]
    steps = tile_ref.shape[0] // CHUNK
    copy = lambda k: pltpu.make_async_copy(
        tile_ref.at[pl.ds(k * CHUNK, CHUNK)], held.at[pl.ds(k % slots * CHUNK, CHUNK)], sems.at[k % slots])

    @pl.loop(0, steps)
    def _(k):
        copy(k).wait()

        @pl.when(k + AHEAD < steps)
        def _():
            copy(k + AHEAD).start()

        for e in range(CHUNK):
            use(k * CHUNK + e, held.at[k % slots * CHUNK + e])


def stream_start(tile_ref, held, sems, first=0, last=AHEAD):
    for k in range(first, last):
        pltpu.make_async_copy(
            tile_ref.at[pl.ds(k * CHUNK, CHUNK)], held.at[pl.ds(k * CHUNK, CHUNK)], sems.at[k]).start()


def stream_scratch(size):
    return [pltpu.VMEM(((AHEAD + 1) * CHUNK, size, size), bf16), pltpu.SemaphoreType.DMA((AHEAD + 1,))]


def degree_kernel(row_ref, count_ref, tile_ref, shift_ref, out_ref, acc, held, sems):
    own, size = shift_ref.shape
    stream_start(tile_ref, held, sems)
    acc[...] = jnp.zeros_like(acc)
    ones = jnp.ones((16, size), bf16)

    def use(t, tile):
        row = jnp.where(t < count_ref[0], row_ref[t], own)
        acc[row] = acc[row] + nt_dot(ones, tile[...])[:8]

    stream(tile_ref, held, sems, use)
    for b in range(own):
        out_ref[b : b + 1, :] = acc[b, 0:1, :] + shift_ref[b : b + 1, :]


def degree_of(tiles, tile_row, tile_count, shift):
    size = tiles.shape[1]
    return call(
        degree_kernel, "degree", [SMEM, SMEM, HBM, shift], [jax.ShapeDtypeStruct(shift.shape, f32)],
        [pltpu.VMEM((shift.shape[0] + 1, 8, size), f32)] + stream_scratch(size), 1.2e10, tiles.size,
    )(tile_row, tile_count, tiles, shift)[0]


def cut_kernel(own, far_index, near_index, place_ref, field_ref, *outs):
    blocks_ref = outs[0]
    size = blocks_ref.shape[2]
    for b in range(own):
        blocks_ref[b] = field_ref[:, b * size : (b + 1) * size]
    nears = outs[1:8]
    pick = nears[0].shape[0]
    for d, near_ref in enumerate(nears, 1):
        mate = (place_ref[0] + d) % (len(nears) + 1)
        for e in range(pick):
            near_ref[e] = blocks_ref[near_index[mate, e]]
    for far_ref in outs[8:]:
        for e in range(far_ref.shape[0]):
            far_ref[e] = blocks_ref[far_index[e]]


def cut(name, own, far_index, near_index, place, field, far):
    width, size = field.shape[0], field.shape[1] // own
    pick = near_index.shape[1]
    shape = lambda n: jax.ShapeDtypeStruct((n, width, size), bf16)
    out = [shape(own)] + [shape(pick)] * 7 + [shape(far_index.shape[0])] * far
    return call(
        functools.partial(cut_kernel, own), name, [SMEM] * 3 + [field], out, [], 0, 8 * field.size,
    )(far_index, near_index, place, field)


def tile_sums(plan, tile_ref, pool, acc, held, sems):
    row_ref, col_ref, count_ref, table_ref = plan
    own = acc.shape[0] - 1

    def use(t, tile):
        row = jnp.where(t < count_ref[0], row_ref[t], own)
        acc[row] = acc[row] + nt_dot(pool[table_ref[col_ref[t]]], tile[...])

    stream(tile_ref, held, sems, use)


def copy_all(pairs, sems):
    copies = [pltpu.make_async_copy(a, b, sems.at[k]) for k, (a, b) in enumerate(pairs)]
    for copy in copies:
        copy.start()
    return copies


def split3(a):
    high = a.astype(bf16)
    rest = a - high.astype(f32)
    mid = rest.astype(bf16)
    return high, mid, (rest - mid.astype(f32)).astype(bf16)


def row_sums(a):
    n = a.shape[0]
    turn = lax.broadcasted_iota(i32, (n, n), 0) == lax.broadcasted_iota(i32, (n, n), 1)
    column = jnp.broadcast_to(jnp.sum(a, axis=1, keepdims=True), (n, n))
    return jnp.sum(jnp.where(turn, column, 0.0), axis=0, keepdims=True)


def first_kernel(*refs):
    plan, far_index, near_index, place_ref = refs[:4], refs[4], refs[5], refs[6]
    tile_ref, own_ref, near_refs, far_ref = refs[7], refs[8], refs[9:16], refs[16]
    degree_ref, p_ref = refs[17:19]
    image_ref, low_ref, send_ref, around_refs = refs[19], refs[20], refs[21], refs[22:29]
    pool, acc, held, sems, pool_sems, ext = refs[29:]
    own, width = own_ref.shape[0], own_ref.shape[1]
    pick = near_refs[0].shape[0]
    pairs = [(own_ref, pool.at[pl.ds(0, own)])]
    pairs += [(ref, pool.at[pl.ds(own + k * pick, pick)]) for k, ref in enumerate(near_refs)]
    pairs += [(far_ref, pool.at[pl.ds(own + 7 * pick, far_ref.shape[0])])]
    copies = copy_all(pairs, pool_sems)
    stream_start(tile_ref, held, sems, 0, 1)
    acc[...] = jnp.zeros_like(acc)
    for copy in copies:
        copy.wait()
    stream_start(tile_ref, held, sems, 1)
    tile_sums(plan, tile_ref, pool, acc, held, sems)
    half = degree_ref.shape[1] // 2
    numer = denom = 0.0
    for b in range(own):
        wide = pool[b].astype(f32)
        image = degree_ref[b : b + 1, :] * wide - acc[b]
        low = image.astype(bf16)
        image_ref[b] = image
        low_ref[b] = low
        for k, part in enumerate((p_ref[b][:, :half], low[:, :half], p_ref[b][:, half:], low[:, half:])):
            ext[b, k * width : (k + 1) * width] = part
        numer = numer + wide * image
        denom = denom + wide * wide
    terms = [jnp.concatenate([u, v], axis=1) for u, v in zip(split3(row_sums(numer)), split3(row_sums(denom)))]
    wide_sums = jnp.concatenate(terms + [jnp.zeros_like(terms[0])], axis=1).astype(f32)
    at = lax.broadcasted_iota(i32, (8, half), 0)
    for b in range(own):
        degree = degree_ref[b : b + 1, :]
        high = degree.astype(bf16).astype(f32)
        tail = jnp.zeros((8, half), f32)
        for k, row in enumerate((high, degree - high, wide_sums)):
            tail = jnp.where(at == 2 * k, row[:, :half], jnp.where(at == 2 * k + 1, row[:, half:], tail))
        ext[b, 4 * width :] = tail.astype(bf16)
    for e in range(send_ref.shape[0]):
        block = far_index[e]
        send_ref[e, 0:width] = ext[block, width : 2 * width]
        send_ref[e, width:] = ext[block, 3 * width :]
    for d, ref in enumerate(around_refs, 1):
        mate = (place_ref[0] + d) % 8
        for e in range(pick):
            ref[e] = ext[near_index[mate, e]]


def op_x(plan, far_index, near_index, place, tiles, own_x, nears, far, degree, p):
    own, width, size = own_x.shape
    pick = nears[0].shape[0]
    blocks = own + 7 * pick + far.shape[0]
    out = [
        jax.ShapeDtypeStruct(own_x.shape, f32),
        jax.ShapeDtypeStruct(own_x.shape, bf16),
        jax.ShapeDtypeStruct((far.shape[0], 2 * width + 8, size // 2), bf16),
    ] + [jax.ShapeDtypeStruct((pick, 4 * width + 8, size // 2), bf16)] * 7
    return call(
        first_kernel, "op_x", [SMEM] * 7 + [HBM] * 10 + [degree, p], out,
        [pltpu.VMEM((blocks, width, size), bf16), pltpu.VMEM((own + 1, width, size), f32)] + stream_scratch(size)
        + [pltpu.SemaphoreType.DMA((9,)), pltpu.VMEM((own, 4 * width + 8, size // 2), bf16)],
        1.2e10, tiles.size,
    )(*plan, far_index, near_index, place, tiles, own_x, *nears, far, degree, p)


def last_kernel(*refs):
    plan, tile_ref = refs[:4], refs[4]
    near_x, near_refs, far_x_ref, far_p_ref, far_ref = refs[5:12], refs[12:19], refs[19], refs[20], refs[21]
    degree_ref, x_ref, p_ref, image_ref, low_x_ref = refs[22:27]
    search_ref, out_ref = refs[27:29]
    pool, acc, held, sems, pool_sems, xs, sent, around = refs[29:]
    own, width, size = x_ref.shape
    pick = near_x[0].shape[0]
    near, far = 7 * pick, far_ref.shape[0]
    pairs = [
        (far_ref, sent),
        (far_x_ref, xs.at[pl.ds(near, far)]),
        (far_p_ref, pool.at[pl.ds(own + near, far), pl.ds(0, width)]),
    ]
    for k in range(7):
        pairs.append((near_x[k], xs.at[pl.ds(k * pick, pick)]))
        pairs.append((near_refs[k], around.at[pl.ds(k * pick, pick)]))
    copies = copy_all(pairs, pool_sems)
    acc[...] = jnp.zeros_like(acc)
    copies[0].wait()
    stream_start(tile_ref, held, sems)

    def add(k, total):
        for e in range(8):
            total = total + sent[k * 8 + e, 2 * width :].astype(f32)
        return total

    sums = lax.fori_loop(0, far // 8, add, jnp.zeros((8, size // 2), f32))
    two = 2 * width
    sums = sums[4:5, :two] + sums[4:5, two:] + sums[5:6, :two]
    ratio = sums[:, :width] / (sums[:, width:two] + 1e-06)
    square = (width, width)
    turn = lax.broadcasted_iota(i32, square, 0) == lax.broadcasted_iota(i32, square, 1)
    ratio = jnp.sum(jnp.where(turn, jnp.broadcast_to(ratio, square), 0.0), axis=1, keepdims=True)

    for b in range(own):
        s = ((image_ref[b] - ratio * x_ref[b].astype(f32)) / degree_ref[b : b + 1, :]).astype(bf16)
        search_ref[b] = s
        pool[b, 0:width] = p_ref[b]
        pool[b, width:] = s
    for copy in copies[1:]:
        copy.wait()

    def join(left, right):
        return jnp.concatenate([left, right], axis=1)

    def form(image, x, tail):
        tail = tail.astype(f32)
        inv = 1.0 / (join(tail[0:1], tail[1:2]) + join(tail[2:3], tail[3:4]))
        return ((image.astype(f32) - ratio * x.astype(f32)) * inv).astype(bf16)

    @pl.loop(0, 7)
    def _(k):
        for e in range(pick):
            m = k * pick + e
            part = lambda r: join(
                around[m, r * width : (r + 1) * width], around[m, (r + 2) * width : (r + 3) * width])
            pool[own + m, 0:width] = part(0)
            pool[own + m, width:] = form(part(1), xs[m], around[m, 4 * width :])

    @pl.loop(0, far // 8)
    def _(k):
        for e in range(8):
            m = k * 8 + e
            low = join(sent[m, 0:width], sent[m, width:two])
            pool[own + near + m, width:] = form(low, xs[near + m], sent[m, two:])

    tile_sums(plan, tile_ref, pool, acc, held, sems)
    total = 0.0
    for b in range(own):
        field = pool[b]
        low = (degree_ref[b : b + 1, :] * field.astype(f32) - acc[b]).astype(bf16)
        basis = jnp.concatenate([x_ref[b], field], axis=0)
        total = total + nt_dot(basis, jnp.concatenate([basis, low_x_ref[b], low], axis=0))
    n = 3 * width
    rest = jnp.concatenate([total[: n // 2, 4 * width :], total[n // 2 :, 4 * width :]], axis=1)
    out_ref[:, 0, :] = jnp.concatenate([total[:, : 4 * width], rest], axis=0).T


def op_ps(plan, tiles, near_x, near, far_x, far_p, far, degree, x, p, image, low_x):
    own, width, size = x.shape
    pick = near_x[0].shape[0]
    count = 7 * pick + far.shape[0]
    n = 3 * width
    out = [jax.ShapeDtypeStruct(x.shape, bf16), jax.ShapeDtypeStruct((4 * width, 1, n + n // 2), f32)]
    return call(
        last_kernel, "op_ps", [SMEM] * 4 + [HBM] * 18 + [degree, x, p, image, low_x], out,
        [pltpu.VMEM((own + count, 2 * width, size), bf16), pltpu.VMEM((own + 1, 2 * width, size), f32)]
        + stream_scratch(size)
        + [
            pltpu.SemaphoreType.DMA((17,)),
            pltpu.VMEM((count, width, size), bf16),
            pltpu.VMEM((far.shape[0], 2 * width + 8, size // 2), bf16),
            pltpu.VMEM((7 * pick, 4 * width + 8, size // 2), bf16),
        ],
        1.2e10, tiles.size,
    )(*plan, tiles, *near_x, *near, far_x, far_p, far, degree, x, p, image, low_x)


def inverse(gram, eye, guess_ref, image_ref):
    root_row = lax.rsqrt(jnp.sum(gram * eye, axis=0, keepdims=True))
    root_col = lax.rsqrt(jnp.sum(gram * eye, axis=1, keepdims=True))
    scaled = gram * root_row * root_col
    bound = jnp.max(jnp.sum(jnp.abs(scaled), axis=1, keepdims=True))
    rough = scaled.astype(bf16)

    def improve(state):
        count, _ = state
        image = image_ref[...]
        guess = exact_dot(guess_ref[...], 2.0 * eye - image)
        guess_ref[...] = guess
        image_ref[...] = exact_dot(scaled, guess)
        return count + 1, jnp.max(jnp.abs(eye - image))

    start = (jnp.int32(0), jnp.float32(1.0))
    guess = eye / bound
    for _ in range(8):
        guess = guess.astype(bf16)
        image = jnp.dot(rough, guess, preferred_element_type=f32)
        guess = jnp.dot(guess, (2.0 * eye - image).astype(bf16), preferred_element_type=f32)
    guess_ref[...] = guess
    image_ref[...] = exact_dot(scaled, guess)
    away = jnp.max(jnp.sum(jnp.abs(eye - image_ref[...]), axis=1, keepdims=True))

    @pl.when(jnp.logical_not(away < 0.9))
    def _():
        guess_ref[...] = eye / bound
        image_ref[...] = scaled / bound

    lax.while_loop(lambda state: (state[1] > 3e-4) & (state[0] < 60), improve, start)
    return exact_dot(guess_ref[...], 2.0 * eye - image_ref[...]) * root_row * root_col


def ritz_kernel(sums_ref, x_ref, p_ref, s_ref, out_x_ref, out_p_ref, guess_ref, image_ref):
    width = x_ref.shape[1]
    n = 3 * width
    eye = (lax.broadcasted_iota(i32, (n, n), 0) == lax.broadcasted_iota(i32, (n, n), 1)).astype(f32)
    sums = sums_ref[:, 0, :].T
    late = sums[n:]
    late = jnp.concatenate([late[:, : 2 * width], late[:, 2 * width :]], axis=0)
    proj = jnp.concatenate([sums[0:n, n:], late], axis=1)
    sym = 0.5 * (proj + proj.T)
    reduced = exact_dot(inverse(sums[0:n, 0:n], eye, guess_ref, image_ref), sym)
    center = jnp.sum(reduced * eye) / n
    moved = reduced - center * eye
    signum = moved * lax.rsqrt(jnp.sum(moved * moved.T) + 1e-06)
    for _ in range(NS):
        square = exact_dot(signum, signum)
        signum = 1.5 * signum - 0.5 * exact_dot(square, signum)
    low_proj = 0.5 * (eye - signum)
    coeff = low_proj.T[:width, :]
    lanes = lax.broadcasted_iota(i32, coeff.shape, 1)
    both = jnp.concatenate([coeff, jnp.where(lanes < width, 0.0, coeff)], axis=0).astype(bf16)
    size = x_ref.shape[2]
    for b in range(out_x_ref.shape[1] // size):
        basis = jnp.concatenate([x_ref[b], p_ref[b], s_ref[b]], axis=0)
        out = jnp.dot(both, basis, preferred_element_type=f32)
        out_x_ref[:, b * size : (b + 1) * size] = out[:width]
        out_p_ref[:, b * size : (b + 1) * size] = out[width:]


def ritz(sums, x, p, search):
    own, width, size = p.shape
    shape = jax.ShapeDtypeStruct((width, own * size), f32)
    return call(
        ritz_kernel, "ritz", [sums, x, p, search], [shape, shape],
        [pltpu.VMEM((3 * width, 3 * width), f32)] * 2, 4e9, 2 * MIB,
    )(sums, x, p, search)


def exchange(a, axes):
    return lax.all_to_all(a, axes, split_axis=0, concat_axis=0, tiled=True)


def spread(a, axis, count):
    return exchange(jnp.broadcast_to(a[None], (count,) + a.shape), axis)


def total(a, devices):
    part = jnp.sum(exchange(a, BOTH), axis=0)
    return spread(part, BOTH, devices)


def pass_on(parts, inner):
    return [
        lax.ppermute(part, "inner", [(k, (k + d) % inner) for k in range(inner)])
        for d, part in enumerate(parts, 1)
    ]


def shards(inner, comm, vec_x, vec_p, diag_shift, tiles, tile_row, tile_col, tile_count, send_near, send_far):
    width = vec_x.shape[0]
    size = tiles.shape[1]
    own = diag_shift.shape[0] // size
    place = lax.axis_index("inner").astype(i32)
    devices = inner * comm
    pick = send_near.shape[2]
    far_index, near_index = send_far.reshape(-1), send_near[0]

    before = (place - jnp.arange(inner, dtype=i32)) % inner
    near_table = own + (before[:, None] - 1) * pick + jnp.arange(pick, dtype=i32)[None, :]
    mine = lax.dynamic_index_in_dim(send_near[0], place, axis=0, keepdims=True)
    near_table = jnp.where(before[:, None] == 0, mine, near_table)
    table = jnp.concatenate([
        jnp.arange(own, dtype=i32),
        near_table.reshape(-1),
        own + (inner - 1) * pick + jnp.arange(devices, dtype=i32),
    ])
    spot = place.reshape(1)

    x, *rest = cut("cut_x", own, far_index, near_index, spot, vec_x, 1)
    far_x = exchange(rest[7], BOTH)
    tile_row, table = lax.optimization_barrier((tile_row, table))
    plan = (tile_row, tile_col, tile_count, table)
    degree = degree_of(tiles, tile_row, tile_count, diag_shift.reshape(own, size))
    late, degree = lax.optimization_barrier((rest[4:7], degree))
    near_x = pass_on(rest[:4] + late, inner)
    p, *rest = cut("cut_p", own, far_index, near_index, spot, vec_p, 1)
    far_p = rest[7]
    p, far_p, late = lax.optimization_barrier((p, far_p, late))
    far_x, near_x, far_p = lax.optimization_barrier((far_x, near_x, far_p))
    far_p = exchange(far_p, BOTH)

    image, low_x, far, *near = op_x(
        plan, far_index, near_index, spot, tiles, x, near_x, far_x, degree, p)
    far, far_p, near = lax.optimization_barrier((far, far_p, near))
    far = exchange(far, BOTH)
    near = pass_on(near, inner)
    search, sums = op_ps(plan, tiles, near_x, near, far_x, far_p, far, degree, x, p, image, low_x)
    return tuple(ritz(total(sums, devices), x, p, search))


def solution(mesh):
    in_specs = (
        P(None, BOTH),
        P(None, BOTH),
        P(BOTH),
        P(BOTH, None, None),
        P(BOTH),
        P(BOTH),
        P(BOTH),
        P(BOTH, None, None),
        P(BOTH, None, None),
    )
    out_specs = (P(None, BOTH), P(None, BOTH))
    run = functools.partial(shards, mesh.shape["inner"], mesh.shape["comm"])
    return jax.shard_map(run, mesh=mesh, in_specs=in_specs, out_specs=out_specs, check_vma=False)
```

```python
import functools

import jax
import jax.numpy as jnp
from jax import lax
from jax.experimental import pallas as pl
from jax.experimental.pallas import tpu as pltpu
from jax.sharding import PartitionSpec as P

NS = 6
CHUNK = 24
AHEAD = 2
LIMIT = 60
BOTH = ("comm", "inner")
MIB = 1 << 20
exact_mode = lax.Precision.HIGHEST
f32, bf16, i32 = jnp.float32, jnp.bfloat16, jnp.int32
NT_DIMS = (((1,), (1,)), ((), ()))
VMEM = pl.BlockSpec(memory_space=pltpu.VMEM)
SMEM = pl.BlockSpec(memory_space=pltpu.SMEM)
HBM = pl.BlockSpec(memory_space=pltpu.HBM)


def nt_dot(a, b):
    return lax.dot_general(a, b, NT_DIMS, preferred_element_type=f32)


def exact_dot(a, b):
    return jnp.dot(a, b, precision=exact_mode, preferred_element_type=f32)


def cost(flops, nbytes):
    return pl.CostEstimate(flops=int(flops), bytes_accessed=int(nbytes), transcendentals=0)


def call(kernel, name, specs, out_shape, scratch, flops, nbytes, limit=LIMIT):
    whole = lambda a: pl.BlockSpec(a.shape, lambda g: (0,) * len(a.shape))
    return pl.pallas_call(
        kernel,
        grid=(1,),
        in_specs=[whole(s) if isinstance(s, (jax.Array, jax.core.Tracer)) else s for s in specs],
        out_specs=[whole(a) for a in out_shape],
        out_shape=out_shape,
        scratch_shapes=scratch,
        compiler_params=pltpu.CompilerParams(vmem_limit_bytes=limit * MIB),
        cost_estimate=cost(flops, nbytes),
        name=name,
    )


def stream(tile_ref, held, sems, use):
    slots = sems.shape[0]
    steps = tile_ref.shape[0] // CHUNK
    copy = lambda k: pltpu.make_async_copy(
        tile_ref.at[pl.ds(k * CHUNK, CHUNK)], held.at[pl.ds(k % slots * CHUNK, CHUNK)], sems.at[k % slots])

    @pl.loop(0, steps)
    def _(k):
        copy(k).wait()

        @pl.when(k + AHEAD < steps)
        def _():
            copy(k + AHEAD).start()

        for e in range(CHUNK):
            use(k * CHUNK + e, held.at[k % slots * CHUNK + e])


def stream_start(tile_ref, held, sems, first=0, last=AHEAD):
    for k in range(first, last):
        pltpu.make_async_copy(
            tile_ref.at[pl.ds(k * CHUNK, CHUNK)], held.at[pl.ds(k * CHUNK, CHUNK)], sems.at[k]).start()


def stream_scratch(size):
    return [pltpu.VMEM(((AHEAD + 1) * CHUNK, size, size), bf16), pltpu.SemaphoreType.DMA((AHEAD + 1,))]


def degree_kernel(row_ref, count_ref, tile_ref, shift_ref, out_ref, acc, held, sems):
    own, size = shift_ref.shape
    stream_start(tile_ref, held, sems)
    acc[...] = jnp.zeros_like(acc)
    ones = jnp.ones((16, size), bf16)

    def use(t, tile):
        row = jnp.where(t < count_ref[0], row_ref[t], own)
        acc[row] = acc[row] + nt_dot(ones, tile[...])[:8]

    stream(tile_ref, held, sems, use)
    for b in range(own):
        out_ref[b : b + 1, :] = acc[b, 0:1, :] + shift_ref[b : b + 1, :]


def degree_of(tiles, tile_row, tile_count, shift):
    size = tiles.shape[1]
    return call(
        degree_kernel, "degree", [SMEM, SMEM, HBM, shift], [jax.ShapeDtypeStruct(shift.shape, f32)],
        [pltpu.VMEM((shift.shape[0] + 1, 8, size), f32)] + stream_scratch(size), 1.2e10, tiles.size,
    )(tile_row, tile_count, tiles, shift)[0]


def cut_kernel(own, far_index, near_index, place_ref, field_ref, blocks_ref, *outs):
    step = pl.program_id(0)
    size = blocks_ref.shape[2]
    nears, far_ref = outs[:7], outs[7]
    pick, count = nears[0].shape[0], far_ref.shape[0]

    @pl.when(step == 0)
    def _():
        for b in range(own):
            blocks_ref[b] = field_ref[:, b * size : (b + 1) * size]
        for d, near_ref in enumerate(nears, 1):
            mate = (place_ref[0] + d) % (len(nears) + 1)
            for e in range(pick):
                near_ref[e] = blocks_ref[near_index[mate, e]]

    for e in range(count):
        far_ref[e] = blocks_ref[far_index[step * count + e]]


def cut(name, own, far_index, near_index, place, field, steps=4):
    width, size = field.shape[0], field.shape[1] // own
    pick, count = near_index.shape[1], far_index.shape[0]
    shape = lambda n: jax.ShapeDtypeStruct((n, width, size), bf16)
    held = lambda n: pl.BlockSpec((n, width, size), lambda g: (0, 0, 0))
    return pl.pallas_call(
        functools.partial(cut_kernel, own),
        grid=(steps,),
        in_specs=[SMEM] * 3 + [pl.BlockSpec(field.shape, lambda g: (0, 0))],
        out_specs=[held(own)] + [held(pick)] * 7 + [pl.BlockSpec((count // steps, width, size), lambda g: (g, 0, 0))],
        out_shape=[shape(own)] + [shape(pick)] * 7 + [shape(count)],
        compiler_params=pltpu.CompilerParams(vmem_limit_bytes=LIMIT * MIB),
        cost_estimate=cost(0, 8 * field.size),
        name=name,
    )(far_index, near_index, place, field)


def tile_sums(plan, tile_ref, pool, acc, held, sems):
    row_ref, col_ref, count_ref, table_ref = plan
    own = acc.shape[0] - 1

    def use(t, tile):
        row = jnp.where(t < count_ref[0], row_ref[t], own)
        acc[row] = acc[row] + nt_dot(pool[table_ref[col_ref[t]]], tile[...])

    stream(tile_ref, held, sems, use)


def copy_all(pairs, sems):
    copies = [pltpu.make_async_copy(a, b, sems.at[k]) for k, (a, b) in enumerate(pairs)]
    for copy in copies:
        copy.start()
    return copies


def split3(a):
    high = a.astype(bf16)
    rest = a - high.astype(f32)
    mid = rest.astype(bf16)
    return high, mid, (rest - mid.astype(f32)).astype(bf16)


def row_sums(a):
    n = a.shape[0]
    turn = lax.broadcasted_iota(i32, (n, n), 0) == lax.broadcasted_iota(i32, (n, n), 1)
    column = jnp.broadcast_to(jnp.sum(a, axis=1, keepdims=True), (n, n))
    return jnp.sum(jnp.where(turn, column, 0.0), axis=0, keepdims=True)


def first_kernel(*refs):
    plan, far_index, near_index, place_ref = refs[:4], refs[4], refs[5], refs[6]
    tile_ref, own_ref, near_refs, far_ref = refs[7], refs[8], refs[9:16], refs[16]
    degree_ref, p_ref = refs[17:19]
    image_ref, low_ref, send_ref, around_refs = refs[19], refs[20], refs[21], refs[22:29]
    pool, acc, held, sems, pool_sems, ext = refs[29:]
    own, width = own_ref.shape[0], own_ref.shape[1]
    pick = near_refs[0].shape[0]
    pairs = [(own_ref, pool.at[pl.ds(0, own)])]
    pairs += [(ref, pool.at[pl.ds(own + k * pick, pick)]) for k, ref in enumerate(near_refs)]
    pairs += [(far_ref, pool.at[pl.ds(own + 7 * pick, far_ref.shape[0])])]
    copies = copy_all(pairs, pool_sems)
    stream_start(tile_ref, held, sems, 0, 1)
    acc[...] = jnp.zeros_like(acc)
    for copy in copies:
        copy.wait()
    stream_start(tile_ref, held, sems, 1)
    tile_sums(plan, tile_ref, pool, acc, held, sems)
    half = degree_ref.shape[1] // 2
    numer = denom = 0.0
    for b in range(own):
        wide = pool[b].astype(f32)
        image = degree_ref[b : b + 1, :] * wide - acc[b]
        low = image.astype(bf16)
        image_ref[b] = image
        low_ref[b] = low
        for k, part in enumerate((p_ref[b][:, :half], low[:, :half], p_ref[b][:, half:], low[:, half:])):
            ext[b, k * width : (k + 1) * width] = part
        numer = numer + wide * image
        denom = denom + wide * wide
    terms = [jnp.concatenate([u, v], axis=1) for u, v in zip(split3(row_sums(numer)), split3(row_sums(denom)))]
    wide_sums = jnp.concatenate(terms + [jnp.zeros_like(terms[0])], axis=1).astype(f32)
    at = lax.broadcasted_iota(i32, (8, half), 0)
    for b in range(own):
        degree = degree_ref[b : b + 1, :]
        high = degree.astype(bf16).astype(f32)
        tail = jnp.zeros((8, half), f32)
        for k, row in enumerate((high, degree - high, wide_sums)):
            tail = jnp.where(at == 2 * k, row[:, :half], jnp.where(at == 2 * k + 1, row[:, half:], tail))
        ext[b, 4 * width :] = tail.astype(bf16)
    for e in range(send_ref.shape[0]):
        block = far_index[e]
        send_ref[e, 0:width] = ext[block, width : 2 * width]
        send_ref[e, width:] = ext[block, 3 * width :]
    for d, ref in enumerate(around_refs, 1):
        mate = (place_ref[0] + d) % 8
        for e in range(pick):
            ref[e] = ext[near_index[mate, e]]


def op_x(plan, far_index, near_index, place, tiles, own_x, nears, far, degree, p):
    own, width, size = own_x.shape
    pick = nears[0].shape[0]
    blocks = own + 7 * pick + far.shape[0]
    out = [
        jax.ShapeDtypeStruct(own_x.shape, f32),
        jax.ShapeDtypeStruct(own_x.shape, bf16),
        jax.ShapeDtypeStruct((far.shape[0], 2 * width + 8, size // 2), bf16),
    ] + [jax.ShapeDtypeStruct((pick, 4 * width + 8, size // 2), bf16)] * 7
    return call(
        first_kernel, "op_x", [SMEM] * 7 + [HBM] * 10 + [degree, p], out,
        [pltpu.VMEM((blocks, width, size), bf16), pltpu.VMEM((own + 1, width, size), f32)] + stream_scratch(size)
        + [pltpu.SemaphoreType.DMA((9,)), pltpu.VMEM((own, 4 * width + 8, size // 2), bf16)],
        1.2e10, tiles.size,
    )(*plan, far_index, near_index, place, tiles, own_x, *nears, far, degree, p)


def last_kernel(*refs):
    plan, tile_ref = refs[:4], refs[4]
    near_x, near_refs, far_x_ref, far_p_ref, far_ref = refs[5:12], refs[12:19], refs[19], refs[20], refs[21]
    degree_ref, x_ref, p_ref, image_ref, low_x_ref = refs[22:27]
    search_ref, out_ref = refs[27:29]
    pool, acc, held, sems, pool_sems, xs, sent, around = refs[29:]
    own, width, size = x_ref.shape
    pick = near_x[0].shape[0]
    near, far = 7 * pick, far_ref.shape[0]
    pairs = [
        (far_ref, sent),
        (far_x_ref, xs.at[pl.ds(near, far)]),
        (far_p_ref, pool.at[pl.ds(own + near, far), pl.ds(0, width)]),
    ]
    for k in range(7):
        pairs.append((near_x[k], xs.at[pl.ds(k * pick, pick)]))
        pairs.append((near_refs[k], around.at[pl.ds(k * pick, pick)]))
    copies = copy_all(pairs, pool_sems)
    acc[...] = jnp.zeros_like(acc)
    copies[0].wait()
    stream_start(tile_ref, held, sems)

    def add(k, total):
        for e in range(8):
            total = total + sent[k * 8 + e, 2 * width :].astype(f32)
        return total

    sums = lax.fori_loop(0, far // 8, add, jnp.zeros((8, size // 2), f32))
    two = 2 * width
    sums = sums[4:5, :two] + sums[4:5, two:] + sums[5:6, :two]
    ratio = sums[:, :width] / (sums[:, width:two] + 1e-06)
    square = (width, width)
    turn = lax.broadcasted_iota(i32, square, 0) == lax.broadcasted_iota(i32, square, 1)
    ratio = jnp.sum(jnp.where(turn, jnp.broadcast_to(ratio, square), 0.0), axis=1, keepdims=True)

    for b in range(own):
        s = ((image_ref[b] - ratio * x_ref[b].astype(f32)) / degree_ref[b : b + 1, :]).astype(bf16)
        search_ref[b] = s
        pool[b, 0:width] = p_ref[b]
        pool[b, width:] = s
    for copy in copies[1:]:
        copy.wait()

    def join(left, right):
        return jnp.concatenate([left, right], axis=1)

    def form(image, x, tail):
        tail = tail.astype(f32)
        inv = 1.0 / (join(tail[0:1], tail[1:2]) + join(tail[2:3], tail[3:4]))
        return ((image.astype(f32) - ratio * x.astype(f32)) * inv).astype(bf16)

    @pl.loop(0, 7)
    def _(k):
        for e in range(pick):
            m = k * pick + e
            part = lambda r: join(
                around[m, r * width : (r + 1) * width], around[m, (r + 2) * width : (r + 3) * width])
            pool[own + m, 0:width] = part(0)
            pool[own + m, width:] = form(part(1), xs[m], around[m, 4 * width :])

    @pl.loop(0, far // 8)
    def _(k):
        for e in range(8):
            m = k * 8 + e
            low = join(sent[m, 0:width], sent[m, width:two])
            pool[own + near + m, width:] = form(low, xs[near + m], sent[m, two:])

    tile_sums(plan, tile_ref, pool, acc, held, sems)
    total = 0.0
    for b in range(own):
        field = pool[b]
        low = (degree_ref[b : b + 1, :] * field.astype(f32) - acc[b]).astype(bf16)
        basis = jnp.concatenate([x_ref[b], field], axis=0)
        total = total + nt_dot(basis, jnp.concatenate([basis, low_x_ref[b], low], axis=0))
    n = 3 * width
    rest = jnp.concatenate([total[: n // 2, 4 * width :], total[n // 2 :, 4 * width :]], axis=1)
    out_ref[:, 0, :] = jnp.concatenate([total[:, : 4 * width], rest], axis=0).T


def op_ps(plan, tiles, near_x, near, far_x, far_p, far, degree, x, p, image, low_x):
    own, width, size = x.shape
    pick = near_x[0].shape[0]
    count = 7 * pick + far.shape[0]
    n = 3 * width
    out = [jax.ShapeDtypeStruct(x.shape, bf16), jax.ShapeDtypeStruct((4 * width, 1, n + n // 2), f32)]
    return call(
        last_kernel, "op_ps", [SMEM] * 4 + [HBM] * 18 + [degree, x, p, image, low_x], out,
        [pltpu.VMEM((own + count, 2 * width, size), bf16), pltpu.VMEM((own + 1, 2 * width, size), f32)]
        + stream_scratch(size)
        + [
            pltpu.SemaphoreType.DMA((17,)),
            pltpu.VMEM((count, width, size), bf16),
            pltpu.VMEM((far.shape[0], 2 * width + 8, size // 2), bf16),
            pltpu.VMEM((7 * pick, 4 * width + 8, size // 2), bf16),
        ],
        1.2e10, tiles.size,
    )(*plan, tiles, *near_x, *near, far_x, far_p, far, degree, x, p, image, low_x)


def inverse(gram, eye, guess_ref, image_ref):
    root_row = lax.rsqrt(jnp.sum(gram * eye, axis=0, keepdims=True))
    root_col = lax.rsqrt(jnp.sum(gram * eye, axis=1, keepdims=True))
    scaled = gram * root_row * root_col
    bound = jnp.max(jnp.sum(jnp.abs(scaled), axis=1, keepdims=True))
    rough = scaled.astype(bf16)

    def improve_roughly(state):
        count, _ = state
        guess = guess_ref[...].astype(bf16)
        image = jnp.dot(rough, guess, preferred_element_type=f32)
        guess_ref[...] = jnp.dot(guess, (2.0 * eye - image).astype(bf16), preferred_element_type=f32)
        return count + 1, jnp.max(jnp.abs(eye - image))

    def improve(state):
        count, _ = state
        image = image_ref[...]
        guess = exact_dot(guess_ref[...], 2.0 * eye - image)
        guess_ref[...] = guess
        image_ref[...] = exact_dot(scaled, guess)
        return count + 1, jnp.max(jnp.abs(eye - image))

    start = (jnp.int32(0), jnp.float32(1.0))
    guess_ref[...] = eye / bound
    lax.while_loop(lambda state: (state[1] > 0.1) & (state[0] < 12), improve_roughly, start)
    image_ref[...] = exact_dot(scaled, guess_ref[...])
    away = jnp.max(jnp.sum(jnp.abs(eye - image_ref[...]), axis=1, keepdims=True))

    @pl.when(jnp.logical_not(away < 0.9))
    def _():
        guess_ref[...] = eye / bound
        image_ref[...] = scaled / bound

    lax.while_loop(lambda state: (state[1] > 3e-4) & (state[0] < 60), improve, start)
    return exact_dot(guess_ref[...], 2.0 * eye - image_ref[...]) * root_row * root_col


def ritz_kernel(sums_ref, x_hbm, p_hbm, s_hbm, out_x_ref, out_p_ref, guess_ref, image_ref, x_ref, p_ref, s_ref, sems):
    copies = copy_all([(x_hbm, x_ref), (p_hbm, p_ref), (s_hbm, s_ref)], sems)
    width = x_ref.shape[1]
    n = 3 * width
    eye = (lax.broadcasted_iota(i32, (n, n), 0) == lax.broadcasted_iota(i32, (n, n), 1)).astype(f32)
    sums = sums_ref[:, 0, :].T
    late = sums[n:]
    late = jnp.concatenate([late[:, : 2 * width], late[:, 2 * width :]], axis=0)
    proj = jnp.concatenate([sums[0:n, n:], late], axis=1)
    sym = 0.5 * (proj + proj.T)
    reduced = exact_dot(inverse(sums[0:n, 0:n], eye, guess_ref, image_ref), sym)
    center = jnp.sum(reduced * eye) / n
    moved = reduced - center * eye
    signum = moved * lax.rsqrt(jnp.sum(moved * moved.T) + 1e-06)
    for _ in range(NS):
        square = exact_dot(signum, signum)
        signum = 1.5 * signum - 0.5 * exact_dot(square, signum)
    low_proj = 0.5 * (eye - signum)
    coeff = low_proj.T[:width, :]
    lanes = lax.broadcasted_iota(i32, coeff.shape, 1)
    both = jnp.concatenate([coeff, jnp.where(lanes < width, 0.0, coeff)], axis=0).astype(bf16)
    size = x_ref.shape[2]
    for copy in copies:
        copy.wait()
    for b in range(out_x_ref.shape[1] // size):
        basis = jnp.concatenate([x_ref[b], p_ref[b], s_ref[b]], axis=0)
        out = jnp.dot(both, basis, preferred_element_type=f32)
        out_x_ref[:, b * size : (b + 1) * size] = out[:width]
        out_p_ref[:, b * size : (b + 1) * size] = out[width:]


def ritz(sums, x, p, search):
    own, width, size = p.shape
    shape = jax.ShapeDtypeStruct((width, own * size), f32)
    return call(
        ritz_kernel, "ritz", [sums, HBM, HBM, HBM], [shape, shape],
        [pltpu.VMEM((3 * width, 3 * width), f32)] * 2
        + [pltpu.VMEM(p.shape, bf16)] * 3 + [pltpu.SemaphoreType.DMA((3,))], 4e9, 2 * MIB,
    )(sums, x, p, search)


def exchange(a, axes):
    return lax.all_to_all(a, axes, split_axis=0, concat_axis=0, tiled=True)


def spread(a, axis, count):
    return exchange(jnp.broadcast_to(a[None], (count,) + a.shape), axis)


def total(a, devices):
    part = jnp.sum(exchange(a, BOTH), axis=0)
    return spread(part, BOTH, devices)


def pass_on(parts, inner):
    return [
        lax.ppermute(part, "inner", [(k, (k + d) % inner) for k in range(inner)])
        for d, part in enumerate(parts, 1)
    ]


def shards(inner, comm, vec_x, vec_p, diag_shift, tiles, tile_row, tile_col, tile_count, send_near, send_far):
    width = vec_x.shape[0]
    size = tiles.shape[1]
    own = diag_shift.shape[0] // size
    place = lax.axis_index("inner").astype(i32)
    devices = inner * comm
    pick = send_near.shape[2]
    far_index, near_index = send_far.reshape(-1), send_near[0]

    before = (place - jnp.arange(inner, dtype=i32)) % inner
    near_table = own + (before[:, None] - 1) * pick + jnp.arange(pick, dtype=i32)[None, :]
    mine = lax.dynamic_index_in_dim(send_near[0], place, axis=0, keepdims=True)
    near_table = jnp.where(before[:, None] == 0, mine, near_table)
    table = jnp.concatenate([
        jnp.arange(own, dtype=i32),
        near_table.reshape(-1),
        own + (inner - 1) * pick + jnp.arange(devices, dtype=i32),
    ])
    spot = place.reshape(1)

    x, *rest = cut("cut_x", own, far_index, near_index, spot, vec_x)
    far_x = exchange(rest[7], BOTH)
    tile_row, table = lax.optimization_barrier((tile_row, table))
    plan = (tile_row, tile_col, tile_count, table)
    degree = degree_of(tiles, tile_row, tile_count, diag_shift.reshape(own, size))
    late, degree = lax.optimization_barrier((rest[4:7], degree))
    near_x = pass_on(rest[:4] + late, inner)
    p, *rest = cut("cut_p", own, far_index, near_index, spot, vec_p)
    far_p = rest[7]
    p, far_p, late = lax.optimization_barrier((p, far_p, late))
    far_x, near_x, far_p = lax.optimization_barrier((far_x, near_x, far_p))
    far_p = exchange(far_p, BOTH)

    image, low_x, far, *near = op_x(
        plan, far_index, near_index, spot, tiles, x, near_x, far_x, degree, p)
    far, far_p, near = lax.optimization_barrier((far, far_p, near))
    far = exchange(far, BOTH)
    near = pass_on(near, inner)
    search, sums = op_ps(plan, tiles, near_x, near, far_x, far_p, far, degree, x, p, image, low_x)
    return tuple(ritz(total(sums, devices), x, p, search))


def solution(mesh):
    in_specs = (
        P(None, BOTH),
        P(None, BOTH),
        P(BOTH),
        P(BOTH, None, None),
        P(BOTH),
        P(BOTH),
        P(BOTH),
        P(BOTH, None, None),
        P(BOTH, None, None),
    )
    out_specs = (P(None, BOTH), P(None, BOTH))
    run = functools.partial(shards, mesh.shape["inner"], mesh.shape["comm"])
    return jax.shard_map(run, mesh=mesh, in_specs=in_specs, out_specs=out_specs, check_vma=False)
```
